256 devices in a mesh: dp: 32 (over y, z), mp: 8 (over x, core).
Axes of the slice: x: 4, y: 4, z: 8, core: 2. Of those that a mesh axis runs over, the one named last changes fastest.
Arguments:
- features: bfloat16 [4096, 4096], P('dp'), may hold values from -6 to 6
- upstream: bfloat16 [4096, 8192], P('dp', 'mp'), may hold values from -0.25 to 0.25
- stats: float32 [32, 8, 512, 512], P('dp', 'mp'), may hold values from -0.5 to 1024000, as said below
- accum: float32 [4096, 8192], P('dp', 'mp'), may hold values from 0.01 to 600, as said below
Outputs:
- new_stats: float32 [32, 8, 512, 512], P('dp', 'mp')
- new_accum: float32 [4096, 8192], P('dp', 'mp')
- update: bfloat16 [4096, 8192], P(None, 'mp')
The draws below stay inside these ranges and needn't reach their ends.
Inputs may be any that keep to these rules, and one draw needn't show every extreme that they name: Each stats[i, g] is symmetric; its diagonal entries are at least 512 and exceed the sum of magnitudes of the other entries of their row. `accum`: every entry is positive.
All inputs are finite; a program needn't handle non-finite values.
Results may differ from the reference program's by a relative error of at most 0.0006.
Values may be sent and summed in bfloat16 or wider, within the bound.
A program may use at most 128 MiB of HBM per device.

```python
import math
import jax
import jax.numpy as jnp
from jax import lax

TOK_DEV = 128
ITERS = 6
BLOCK = 512
COLS = 1024
D = 4096
OWNERS = 32
GROUPS = 8
TOKENS = 4096
N_DP = 32


def draw_stats(key, part):
    key = jax.random.fold_in(key, 7)
    noise_key, level_key = jax.random.split(key, 2)
    full_shape = (OWNERS, GROUPS, BLOCK, BLOCK)
    noise = jax.random.uniform(noise_key, full_shape, jnp.float32, -1.0, 1.0)
    symmetric = 0.25 * (noise + jnp.swapaxes(noise, -1, -2))
    levels = jnp.exp(jax.random.uniform(level_key, (OWNERS, GROUPS, BLOCK), jnp.float32, 0.0, math.log(2000.0)))
    identity = jnp.eye(BLOCK, dtype=jnp.float32)
    diagonal = BLOCK * levels
    return symmetric * (1.0 - identity) + identity * diagonal[..., :, None]


def draw_accum(key, part):
    key = jax.random.fold_in(key, 11)
    total_cols = COLS * GROUPS
    row_place = jnp.arange(D, dtype=jnp.float32)[:, None] / D
    col_place = jnp.arange(total_cols, dtype=jnp.float32)[None, :] / total_cols
    base = 0.1 * jnp.exp(row_place * math.log(100.0) + col_place * math.log(3.0))
    jitter = jnp.exp(jax.random.uniform(key, (D, total_cols), jnp.float32, math.log(0.5), math.log(2.0)))
    return base * jitter


def level_of(rng, shape, cuts, least, largest):
    def one(position, parts):
        heights = jax.random.uniform(jax.random.fold_in(jax.random.fold_in(rng, 6), position), (parts,), jnp.float32, least / len(cuts), largest / len(cuts))
        return jnp.repeat(jnp.exp(heights), shape[position] // parts).reshape((-1,) + (1,) * (len(shape) - position - 1))

    gain = one(*cuts[0])
    for cut in cuts[1:]:
        gain = gain * one(*cut)
    return gain


def gaussian(rng, extent, spread, most, cuts=(), held_as=jnp.bfloat16):
    loudness = level_of(rng, extent, cuts, -0.22, 0.18) if cuts else 1.0
    result = jax.random.normal(rng, extent, jnp.float32) * spread * loudness
    return jnp.minimum(jnp.maximum(result, -most), most).astype(held_as)


def setup_inputs(seed: int = 0) -> dict:
    key_list = jax.random.split(jax.random.key(seed), 5)
    return {
        "features": gaussian(key_list[0], (TOKENS, D), 1.0, 6.0, ((0, 32),)),
        "upstream": gaussian(key_list[1], (TOKENS, COLS * GROUPS), (1.0 / (TOK_DEV * N_DP) ** 0.5), 0.25, ((0, 32), (1, 8))),
        "stats": draw_stats(jax.random.fold_in(key_list[4], 71), 0),
        "accum": draw_accum(jax.random.fold_in(key_list[4], 71), 0),
    }


def matmul(first, second):
    return jnp.matmul(first, second, precision=lax.Precision.HIGHEST)

def newton_root(stat):
    identity = jnp.eye(stat.shape[-1], dtype=jnp.float32)
    factor = 2.5 / jnp.sqrt(lax.optimization_barrier(jnp.sum(stat * stat, axis=(-2, -1), keepdims=True)))
    iterate = identity * factor ** 0.25
    coupled = stat * factor
    for iteration in range(ITERS):
        step_factor = (5.0 * identity - coupled) * 0.25
        iterate = matmul(iterate, step_factor)
        if iteration + 1 < ITERS:
            squared = matmul(step_factor, step_factor)
            coupled = matmul(squared, matmul(squared, coupled))
    return iterate

def reference(features, upstream, stats, accum):
    gradient = jnp.dot(features.T, upstream, preferred_element_type=jnp.float32)
    new_accum = accum + gradient * gradient
    adagrad = gradient / jnp.sqrt(new_accum)
    row_blocks = D // BLOCK

    def one_group(group_index):
        group_cols = lax.dynamic_slice_in_dim(gradient, group_index * COLS, COLS, 1)
        blocks = group_cols.reshape(row_blocks, BLOCK, 2, BLOCK).transpose(0, 2, 1, 3).reshape(2 * row_blocks, BLOCK, BLOCK)
        group_stats = lax.dynamic_index_in_dim(stats, group_index, 1, keepdims=False)
        paired = group_stats.reshape(2 * row_blocks, 2, BLOCK, BLOCK)
        flipped = jnp.swapaxes(blocks, 1, 2)
        left_stat = paired[:, 0] + matmul(blocks, flipped)
        right_stat = paired[:, 1] + matmul(flipped, blocks)
        new_group = jnp.stack([left_stat, right_stat], 1).reshape(OWNERS, BLOCK, BLOCK)
        left_root = newton_root(left_stat)
        right_root = newton_root(right_stat)
        precond = matmul(matmul(left_root, blocks), right_root)
        precond = precond.reshape(row_blocks, 2, BLOCK, BLOCK).transpose(0, 2, 1, 3).reshape(D, COLS)
        return (new_group, precond)
    new_groups, precond = lax.map(one_group, jnp.arange(GROUPS, dtype=jnp.int32))
    new_stats = jnp.transpose(new_groups, (1, 0, 2, 3))
    precond = jnp.transpose(precond, (1, 0, 2)).reshape(D, GROUPS * COLS)
    adagrad_total = jnp.sum(adagrad * adagrad)
    precond_total = jnp.sum(precond * precond)
    update = (precond * jnp.sqrt(adagrad_total / (precond_total + 1e-12))).astype(jnp.bfloat16)
    return (new_stats, new_accum, update)
```

```python
import functools

import jax
import jax.numpy as jnp
from jax import lax
from jax.experimental import pallas as pl
from jax.experimental.pallas import tpu as pltpu
from jax.sharding import PartitionSpec as P

ITERS = 6
NX, NY, NZ, NC = 4, 4, 8, 2
MESH = pl.DeviceIdType.MESH
BLOCK = 512
HALF = BLOCK // 2
ROWS_A = 96
ROWS_B = HALF - ROWS_A


def place():
    dp, mp = lax.axis_index("dp"), lax.axis_index("mp")
    return mp // NC, dp // NZ, dp % NZ, mp % NC


def device(x, y, z, core):
    return (y * NZ + z, x * NC + core)


def wrap(value, size):
    return lax.rem(value + size, size)


def greet(partners):
    barrier = pltpu.get_barrier_semaphore()
    for partner in partners:
        pl.semaphore_signal(barrier, inc=1, device_id=partner, device_id_type=MESH)
    pl.semaphore_wait(barrier, len(partners))


def remote(src, dst, send_sem, recv_sem, target):
    return pltpu.make_async_remote_copy(
        src_ref=src,
        dst_ref=dst,
        send_sem=send_sem,
        recv_sem=recv_sem,
        device_id=target,
        device_id_type=MESH,
    )


Z_ORDER = (0, 1, 7, 2, 6, 3, 5, 4)


def gather_kernel(
    features, upstream, f_out, u_out, f_y,
    fy_send, fy_recv, fz_send, fz_recv, fx_send, fx_recv,
    uz_send, uz_recv, uy_send, uy_recv, local_sem,
):
    x, y, z, core = place()
    partners = [device(wrap(x + 1, NX), y, z, core), device(wrap(x - 1, NX), y, z, core)]
    partners += [device(x, wrap(y + a, NY), z, core) for a in range(1, NY)]
    partners += [device(x, y, wrap(z + d, NZ), c) for d in range(1, NZ) for c in range(NC)]
    partners += [device(x, y, z, 1 - core)]
    greet(partners)

    sends = []

    def go(copy):
        copy.start()
        sends.append(copy)

    up, down = wrap(y + 1, NY), wrap(y - 1, NY)
    right, left = wrap(x + 1, NX), wrap(x - 1, NX)

    my_tokens = pl.ds(pl.multiple_of(64 * core + 16 * x, 16), 16)

    def f_cols(row):
        return features.at[my_tokens, pl.ds(pl.multiple_of(row * 1024, 1024), 1024)]

    for a in (2, 1, 3):
        row = wrap(y + a, NY)
        go(remote(f_cols(row), f_y.at[y], fy_send.at[a], fy_recv.at[a], device(x, row, z, core)))
    f_own = pltpu.make_async_copy(f_cols(y), f_y.at[y], local_sem.at[0])
    f_own.start()

    parity = wrap(core - z % NC, NC)

    def u_tile(token_half, row):
        column = pl.multiple_of((row // 2) % 2 * BLOCK, BLOCK)
        return upstream.at[pl.ds(64 * token_half, 64), pl.ds(column, BLOCK)]

    here = parity == 0
    for j in (2, 1, 3, 0):
        d = 2 * j + parity
        row = wrap(z + d, NZ)
        for c in range(NC):
            copy = remote(
                u_tile(c, row), u_out.at[y, z], uz_send.at[j, c], uz_recv.at[d], device(x, y, row, c)
            )
            if j == 0:
                mine = here & (core == c)

                @pl.when(mine)
                def _():
                    pltpu.make_async_copy(u_tile(c, z), u_out.at[y, z], local_sem.at[1]).start()

                @pl.when(jnp.logical_not(mine))
                def _():
                    copy.start()
            else:
                go(copy)

    f_own.wait()
    for a in (1, 3, 2):
        origin = wrap(y - a, NY)
        remote(f_cols(y), f_y.at[origin], fy_send.at[a], fy_recv.at[a], device(x, y, z, core)).wait_recv()

    def f_half(row):
        return f_y.at[:, :, pl.ds(pl.multiple_of(row // 4 * BLOCK, BLOCK), BLOCK)]

    for d in (4, 3, 5, 2, 6, 1, 7):
        row = wrap(z + d, NZ)
        go(
            remote(
                f_half(row), f_out.at[:, z, x], fz_send.at[d], fz_recv.at[d], device(x, y, row, core)
            )
        )
    f_keep = pltpu.make_async_copy(f_half(z), f_out.at[:, z, x], local_sem.at[2])
    f_keep.start()

    def u_part(row, origin, part):
        ref = u_out.at[row, origin]
        return ref if part is None else ref.at[pl.ds(32 * part, 32), :]

    def send_u(origin, d, slot, row, part, forward_to):
        ref = u_part(row, origin, part)
        go(remote(ref, ref, uy_send.at[d, slot], uy_recv.at[d, slot], device(x, forward_to, z, core)))

    def wait_u(origin, d, slot, row, part):
        ref = u_part(row, origin, part)
        remote(ref, ref, uy_send.at[d, slot], uy_recv.at[d, slot], device(x, up, z, core)).wait_recv()

    def f_part(column, origin, part):
        return f_out.at[:, origin, column] if part is None else f_out.at[pl.ds(2 * part, 2), origin, column]

    def send_f(origin, d, slot, column, part, forward_to):
        ref = f_part(column, origin, part)
        go(remote(ref, ref, fx_send.at[d, slot], fx_recv.at[d, slot], device(forward_to, y, z, core)))

    def wait_f(origin, d, slot, column, part):
        ref = f_part(column, origin, part)
        remote(ref, ref, fx_send.at[d, slot], fx_recv.at[d, slot], device(right, y, z, core)).wait_recv()

    def u_first(d):
        origin = wrap(z - d, NZ)
        ref = u_out.at[y, origin]
        arrived = remote(ref, ref, uz_send.at[0, 0], uz_recv.at[d], device(x, y, z, core))
        if d == 0:
            mine = z % NC == core

            @pl.when(mine)
            def _():
                pltpu.make_async_copy(ref, ref, local_sem.at[1]).wait()

            @pl.when(jnp.logical_not(mine))
            def _():
                arrived.wait_recv()
        else:
            arrived.wait_recv()
        send_u(origin, d, 0, y, None, up)
        send_u(origin, d, 1, y, None, down)

    def u_second(d):
        origin = wrap(z - d, NZ)
        wait_u(origin, d, 0, down, None)
        send_u(origin, d, 2, down, 0, up)
        wait_u(origin, d, 1, up, None)
        send_u(origin, d, 3, up, 1, down)

    def u_last(d):
        origin = wrap(z - d, NZ)
        far = wrap(y + 2, NY)
        wait_u(origin, d, 2, far, 0)
        wait_u(origin, d, 3, far, 1)

    def f_first(d):
        origin = wrap(z - d, NZ)
        ref = f_out.at[:, origin, x]
        if d == 0:
            f_keep.wait()
        else:
            remote(ref, ref, fz_send.at[d], fz_recv.at[d], device(x, y, z, core)).wait_recv()
        send_f(origin, d, 0, x, None, right)
        send_f(origin, d, 1, x, None, left)

    def f_second(d):
        origin = wrap(z - d, NZ)
        wait_f(origin, d, 0, left, None)
        send_f(origin, d, 2, left, 0, right)
        wait_f(origin, d, 1, right, None)
        send_f(origin, d, 3, right, 1, left)

    def f_last(d):
        origin = wrap(z - d, NZ)
        far = wrap(x + 2, NX)
        wait_f(origin, d, 2, far, 0)
        wait_f(origin, d, 3, far, 1)

    f_first(0)
    for step in range(NZ + 3):
        if step < NZ:
            u_first(Z_ORDER[step])
        if 1 <= step <= NZ - 1:
            f_first(Z_ORDER[step])
        if 1 <= step <= NZ:
            u_second(Z_ORDER[step - 1])
        if 2 <= step <= NZ + 1:
            f_second(Z_ORDER[step - 2])
        if 2 <= step <= NZ + 1:
            u_last(Z_ORDER[step - 2])
        if 3 <= step <= NZ + 2:
            f_last(Z_ORDER[step - 3])

    for copy in sends:
        copy.wait_send()
    for c in range(NC):
        @pl.when(jnp.logical_not(here & (core == c)))
        def _():
            remote(
                u_tile(c, z), u_out.at[y, z], uz_send.at[0, c], uz_recv.at[0], device(x, y, z, 1 - core)
            ).wait_send()


def gather_inputs(features, upstream):
    dma = pltpu.SemaphoreType.DMA
    f_all, u_all = pl.pallas_call(
        gather_kernel,
        out_shape=(
            jax.ShapeDtypeStruct((NY, NZ, NX, 16, BLOCK), jnp.bfloat16),
            jax.ShapeDtypeStruct((NY, NZ, 64, BLOCK), jnp.bfloat16),
        ),
        in_specs=[pl.BlockSpec(memory_space=pl.ANY)] * 2,
        out_specs=(pl.BlockSpec(memory_space=pl.ANY),) * 2,
        scratch_shapes=[
            pltpu.VMEM((NY, 16, 1024), jnp.bfloat16),
            dma((NY,)), dma((NY,)), dma((NZ,)), dma((NZ,)), dma((NZ, 4)), dma((NZ, 4)),
            dma((4, NC)), dma((NZ,)), dma((NZ, 4)), dma((NZ, 4)), dma((3,)),
        ],
        compiler_params=pltpu.CompilerParams(collective_id=0, has_side_effects=True),
    )(features, upstream)
    return f_all.reshape(-1, BLOCK), u_all.reshape(-1, BLOCK)


def spread_plan():
    rows = (ROWS_A, ROWS_B)
    first, second = (0, 1), (1, 0)
    sizes = (NY, NZ)

    def onward(part):
        kind, offsets, half = part
        out = []
        for level, axis in enumerate((first, second)[kind]):
            far = sizes[axis] // 2
            offset = offsets[axis]
            later = (first, second)[kind][level + 1 :]
            if any(offsets[other] != 0 for other in later):
                continue
            for sign in (1, -1):
                if offset * sign > 0 or abs(offset) == far:
                    continue
                moved = list(offsets)
                moved[axis] = offset - sign
                if abs(moved[axis]) == far:
                    moved[axis] = far
                    out.append((axis, sign, (kind, tuple(moved), 0 if sign == 1 else 1)))
                else:
                    out.append((axis, sign, (kind, tuple(moved), None)))
        return out

    return rows, onward


def spread_schedule():
    rows, onward = spread_plan()
    link_free = {}
    events = []
    pending = []
    halves = {}

    def launch(time, part):
        sends = []
        for axis, sign, moved in onward(part):
            count = rows[moved[0]] // (1 if moved[2] is None else 2)
            begin = max(time, link_free.get((axis, sign), 0.0))
            done = begin + count * BLOCK * 2 * 2 / 100e3
            link_free[(axis, sign)] = done
            pending.append((done + 1.0, len(pending), moved))
            sends.append((axis, sign, moved))
        return sends

    start = [launch(0.0, (kind, (0, 0), None)) for kind in (1, 0)]
    while pending:
        pending.sort()
        time, _, part = pending.pop(0)
        kind, offsets, half = part
        if half is not None:
            halves[(kind, offsets)] = halves.get((kind, offsets), 0) + 1
            if halves[(kind, offsets)] == 2:
                events.append((part, launch(time, (kind, offsets, None))))
            else:
                events.append((part, []))
        else:
            events.append((part, launch(time, part)))
    return [send for group in start for send in group], events


def spread_kernel(
    block, sums, out, other_block, shard, mp_sums, y_sums, z_sums, mp_total, y_total,
    mp_send, mp_recv, ys_send, ys_recv, zs_send, zs_recv, swap_sem, send_sem, recv_sem, local_sem,
):
    x, y, z, core = place()
    mp = x * NC + core
    mp_peers = [(y * NZ + z, wrap(mp + j, NX * NC)) for j in range(1, NX * NC)]
    y_peers = [device(x, wrap(y + j, NY), z, core) for j in range(1, NY)]
    z_peers = [device(x, y, wrap(z + j, NZ), core) for j in range(1, NZ)]
    swapped = z % NC != core
    swap_peer = device(x, y, z + 1 - 2 * (z % NC), 1 - core)
    greet(mp_peers + y_peers + z_peers + [swap_peer])

    swap = remote(block, other_block, swap_sem.at[0], swap_sem.at[1], swap_peer)

    @pl.when(swapped)
    def _():
        swap.start()

    def reduce_over(peers, source, slots, sends, recvs):
        copies = [
            remote(source, slots.at[j], sends.at[j], recvs.at[j], peer) for j, peer in enumerate(peers)
        ]
        for copy in copies:
            copy.start()
        total = source[...]
        for j, copy in enumerate(copies):
            copy.wait_recv()
            total = total + slots[j]
        return total, copies

    total, sent_mp = reduce_over(mp_peers, sums, mp_sums, mp_send, mp_recv)
    mp_total[...] = total
    total, sent_y = reduce_over(y_peers, mp_total, y_sums, ys_send, ys_recv)
    y_total[...] = total
    total, sent_z = reduce_over(z_peers, y_total, z_sums, zs_send, zs_recv)
    scale = jnp.sqrt(total[0:1, 0:1] / (total[1:2, 0:1] + 1e-12))

    @pl.when(swapped)
    def _():
        swap.wait()
        shard[...] = (other_block[...] * scale).astype(jnp.bfloat16)

    @pl.when(jnp.logical_not(swapped))
    def _():
        shard[...] = (block[...] * scale).astype(jnp.bfloat16)

    first_row, row_count = (0, ROWS_A), (ROWS_A, ROWS_B)

    def region(part):
        kind, (a, b), half = part
        row, depth = wrap(y + a, NY), wrap(z + b, NZ)
        count = row_count[kind]
        begin = row * 1024 + depth // 4 * BLOCK + depth % 2 * HALF + first_row[kind]
        if half is not None:
            count //= 2
            begin = begin + half * count
        column = pl.multiple_of((depth // 2) % 2 * BLOCK, BLOCK)
        return out.at[pl.ds(pl.multiple_of(begin, 16), count), pl.ds(column, BLOCK)]

    start, events = spread_schedule()
    keys = [part for part, _ in events]
    sent = []

    def send(axis, sign, moved):
        kind, offsets, half = moved
        mine = list(offsets)
        mine[axis] += sign
        if offsets[axis] == (NY, NZ)[axis] // 2:
            mine[axis] = sign * offsets[axis] * -1 + sign
        mine = tuple(mine)
        here = region((kind, mine, half))
        if mine == (0, 0):
            count = row_count[kind] // (1 if half is None else 2)
            source = shard.at[pl.ds(first_row[kind] + (half or 0) * count, count), :]
        else:
            source = here
        target = (
            device(x, wrap(y + sign, NY), z, core) if axis == 0 else device(x, y, wrap(z + sign, NZ), core)
        )
        index = keys.index(moved)
        copy = remote(source, here, send_sem.at[index], recv_sem.at[index], target)
        copy.start()
        sent.append(copy)

    for one in start:
        send(*one)
    whole = pltpu.make_async_copy(
        shard,
        out.at[
            pl.ds(pl.multiple_of(y * 1024 + z // 4 * BLOCK + z % 2 * HALF, HALF), HALF),
            pl.ds(pl.multiple_of((z // 2) % 2 * BLOCK, BLOCK), BLOCK),
        ],
        local_sem.at[0],
    )
    whole.start()
    for index, (part, onward) in enumerate(events):
        here = region(part)
        remote(here, here, send_sem.at[index], recv_sem.at[index], swap_peer).wait_recv()
        for one in onward:
            send(*one)
    for copy in sent + sent_mp + sent_y + sent_z:
        copy.wait_send()
    whole.wait()


def spread_update(block, sums):
    dma = pltpu.SemaphoreType.DMA
    tile = (8, 128)
    count = len(spread_schedule()[1])
    return pl.pallas_call(
        spread_kernel,
        out_shape=jax.ShapeDtypeStruct((NY * NZ * 128, 1024), jnp.bfloat16),
        in_specs=[pl.BlockSpec(memory_space=pltpu.VMEM)] * 2,
        out_specs=pl.BlockSpec(memory_space=pl.ANY),
        scratch_shapes=[
            pltpu.VMEM((HALF, BLOCK), jnp.float32),
            pltpu.VMEM((HALF, BLOCK), jnp.bfloat16),
            pltpu.VMEM((NX * NC, *tile), jnp.float32),
            pltpu.VMEM((NY, *tile), jnp.float32),
            pltpu.VMEM((NZ, *tile), jnp.float32),
            pltpu.VMEM(tile, jnp.float32),
            pltpu.VMEM(tile, jnp.float32),
            dma((NX * NC,)), dma((NX * NC,)), dma((NY,)), dma((NY,)), dma((NZ,)), dma((NZ,)),
            dma((2,)), dma((count,)), dma((count,)), dma((1,)),
        ],
        compiler_params=pltpu.CompilerParams(collective_id=1, has_side_effects=True),
    )(block, sums)


def product(first, second, dims=(1, 0)):
    return lax.dot_general(
        first,
        second,
        (((dims[0],), (dims[1],)), ((), ())),
        precision=lax.Precision.HIGH,
        preferred_element_type=jnp.float32,
    )


def newton_root(stat):
    identity = jnp.eye(stat.shape[-1], dtype=jnp.float32)
    factor = 2.5 / jnp.sqrt(jnp.sum(stat * stat, axis=(-2, -1), keepdims=True))
    iterate = None
    coupled = stat * factor
    for iteration in range(ITERS):
        step_factor = (5.0 * identity - coupled) * 0.25
        iterate = factor**0.25 * step_factor if iterate is None else product(iterate, step_factor)
        if iteration + 1 < ITERS:
            squared = product(step_factor, step_factor)
            coupled = product(squared, product(squared, coupled))
    return iterate


def index_of(y, z, x, core):
    return (y * NZ + z) * NX * NC + x * NC + core


def every():
    return [(y, z, x) for y in range(NY) for z in range(NZ) for x in range(NX)]


BOTH = ("dp", "mp")
SWAP = [
    (index_of(y, z, x, core), index_of(y, z ^ 1, x, 1 - core))
    for y, z, x in every()
    for core in range(NC)
    if z % 2 != core
]
CORES = [
    (index_of(y, z, x, core), index_of(y, z, x, 1 - core)) for y, z, x in every() for core in range(NC)
]


def shards(features, upstream, stats, accum):
    x, y, z, core = place()
    member = z % 4
    swapped = z % NC != core
    left_side = core == 0
    other_stat = lax.ppermute(stats[0, 0], BOTH, SWAP)
    f_all, u_all = gather_inputs(features, upstream)
    over_tokens = functools.partial(
        lax.dot_general,
        dimension_numbers=(((0,), (0,)), ((), ())),
        preferred_element_type=jnp.float32,
    )
    straight, turned = over_tokens(f_all, u_all), over_tokens(u_all, f_all)
    mine = jnp.where(left_side, straight, turned)
    block = mine + lax.ppermute(jnp.where(left_side, turned, straight), BOTH, CORES)

    pieces = []
    for turn in range(4):
        rows = lax.dynamic_slice_in_dim(block, (member + turn) % 4 * 128, 128, 0)
        perm = [
            (index_of(y, z, x, 0), index_of(y, z // 4 * 4 + (z + turn) % 4, x, z % 2)) for y, z, x in every()
        ]
        pieces.append(lax.ppermute(rows, BOTH, perm))
    near, far = pieces[0] + pieces[1], pieces[2] + pieces[3]
    near_first = wrap(member - wrap(member - core, 2), 4) // 2 == 0
    gradient = jnp.concatenate(
        [jnp.where(near_first, near, far), jnp.where(near_first, far, near)], 1
    )
    new_accum = accum + gradient * gradient
    adagrad = gradient / jnp.sqrt(new_accum)

    new_stat = jnp.where(swapped, other_stat, stats[0, 0]) + product(block, block, (1, 1))
    stat_back = lax.ppermute(new_stat, BOTH, SWAP)
    root = newton_root(new_stat)
    other_root = lax.ppermute(root, BOTH, CORES)
    left_root, right_root = jnp.where(left_side, root, other_root), jnp.where(left_side, other_root, root)
    left_rows = lax.dynamic_slice_in_dim(left_root, core * HALF, HALF, 0)
    straight_block = jnp.where(left_side, block, block.T)
    precond = product(product(left_rows, straight_block), right_root)

    totals = jnp.where(
        lax.broadcasted_iota(jnp.int32, (8, 128), 0) == 0, jnp.sum(adagrad * adagrad), jnp.sum(precond * precond)
    )
    update = spread_update(precond, totals)
    return (jnp.where(swapped, stat_back, new_stat)[None, None], new_accum, update)


def solution(mesh):
    placed = (P("dp", None), P("dp", "mp"), P("dp", "mp", None, None), P("dp", "mp"))
    return jax.shard_map(
        shards,
        mesh=mesh,
        in_specs=placed,
        out_specs=(P("dp", "mp", None, None), P("dp", "mp"), P(None, "mp")),
        check_vma=False,
    )
```

```python
import functools

import jax
import jax.numpy as jnp
from jax import lax
from jax.experimental import pallas as pl
from jax.experimental.pallas import tpu as pltpu
from jax.sharding import PartitionSpec as P

ITERS = 6
NX, NY, NZ, NC = 4, 4, 8, 2
MESH = pl.DeviceIdType.MESH
BLOCK = 512
HALF = BLOCK // 2
ROWS_A = 96
ROWS_B = HALF - ROWS_A


def place():
    dp, mp = lax.axis_index("dp"), lax.axis_index("mp")
    return mp // NC, dp // NZ, dp % NZ, mp % NC


def device(x, y, z, core):
    return (y * NZ + z, x * NC + core)


def wrap(value, size):
    return lax.rem(value + size, size)


def greet(partners):
    barrier = pltpu.get_barrier_semaphore()
    for partner in partners:
        pl.semaphore_signal(barrier, inc=1, device_id=partner, device_id_type=MESH)
    pl.semaphore_wait(barrier, len(partners))


def remote(src, dst, send_sem, recv_sem, target):
    return pltpu.make_async_remote_copy(
        src_ref=src,
        dst_ref=dst,
        send_sem=send_sem,
        recv_sem=recv_sem,
        device_id=target,
        device_id_type=MESH,
    )


Z_ORDER = (0, 1, 7, 2, 6, 3, 5, 4)


def gather_kernel(
    features, upstream, stats, f_out, u_out, stat_out, f_y, stat_send, stat_recv,
    fy_send, fy_recv, fz_send, fz_recv, fx_send, fx_recv,
    uz_send, uz_recv, uy_send, uy_recv, local_sem,
):
    x, y, z, core = place()
    partners = [device(wrap(x + 1, NX), y, z, core), device(wrap(x - 1, NX), y, z, core)]
    partners += [device(x, wrap(y + a, NY), z, core) for a in range(1, NY)]
    partners += [device(x, y, wrap(z + d, NZ), c) for d in range(1, NZ) for c in range(NC)]
    partners += [device(x, y, z, 1 - core)]
    greet(partners)

    sends = []

    def go(copy):
        copy.start()
        sends.append(copy)

    up, down = wrap(y + 1, NY), wrap(y - 1, NY)
    right, left = wrap(x + 1, NX), wrap(x - 1, NX)

    swapped = z % NC != core

    def stat_rows(i):
        return pl.ds(128 * i, 128), pl.ds(128 * i, BLOCK - 128 * i)

    stat_copies = [
        remote(
            stats.at[stat_rows(i)],
            stat_out.at[stat_rows(i)],
            stat_send.at[i],
            stat_recv.at[i],
            device(x, y, z + 1 - 2 * (z % NC), 1 - core),
        )
        for i in range(4)
    ]
    stat_keep = pltpu.make_async_copy(stats, stat_out, local_sem.at[3])

    my_tokens = pl.ds(pl.multiple_of(64 * core + 16 * x, 16), 16)

    def f_cols(row):
        return features.at[my_tokens, pl.ds(pl.multiple_of(row * 1024, 1024), 1024)]

    for a in (2, 1, 3):
        row = wrap(y + a, NY)
        go(remote(f_cols(row), f_y.at[y], fy_send.at[a], fy_recv.at[a], device(x, row, z, core)))
    f_own = pltpu.make_async_copy(f_cols(y), f_y.at[y], local_sem.at[0])
    f_own.start()

    parity = wrap(core - z % NC, NC)

    def u_tile(token_half, row):
        column = pl.multiple_of((row // 2) % 2 * BLOCK, BLOCK)
        return upstream.at[pl.ds(64 * token_half, 64), pl.ds(column, BLOCK)]

    here = parity == 0
    for j in (2, 1, 3, 0):
        d = 2 * j + parity
        row = wrap(z + d, NZ)
        for c in range(NC):
            copy = remote(
                u_tile(c, row), u_out.at[y, z], uz_send.at[j, c], uz_recv.at[d], device(x, y, row, c)
            )
            if j == 0:
                mine = here & (core == c)

                @pl.when(mine)
                def _():
                    pltpu.make_async_copy(u_tile(c, z), u_out.at[y, z], local_sem.at[1]).start()

                @pl.when(jnp.logical_not(mine))
                def _():
                    copy.start()
            else:
                go(copy)

    @pl.when(swapped)
    def _():
        for copy in stat_copies:
            copy.start()

    @pl.when(jnp.logical_not(swapped))
    def _():
        stat_keep.start()

    f_own.wait()
    for a in (1, 3, 2):
        origin = wrap(y - a, NY)
        remote(f_cols(y), f_y.at[origin], fy_send.at[a], fy_recv.at[a], device(x, y, z, core)).wait_recv()

    def f_half(row):
        return f_y.at[:, :, pl.ds(pl.multiple_of(row // 4 * BLOCK, BLOCK), BLOCK)]

    for d in (4, 3, 5, 2, 6, 1, 7):
        row = wrap(z + d, NZ)
        go(
            remote(
                f_half(row), f_out.at[:, z, x], fz_send.at[d], fz_recv.at[d], device(x, y, row, core)
            )
        )
    f_keep = pltpu.make_async_copy(f_half(z), f_out.at[:, z, x], local_sem.at[2])
    f_keep.start()

    def u_part(row, origin, part):
        ref = u_out.at[row, origin]
        return ref if part is None else ref.at[pl.ds(32 * part, 32), :]

    def send_u(origin, d, slot, row, part, forward_to):
        ref = u_part(row, origin, part)
        go(remote(ref, ref, uy_send.at[d, slot], uy_recv.at[d, slot], device(x, forward_to, z, core)))

    def wait_u(origin, d, slot, row, part):
        ref = u_part(row, origin, part)
        remote(ref, ref, uy_send.at[d, slot], uy_recv.at[d, slot], device(x, up, z, core)).wait_recv()

    def f_part(column, origin, part):
        return f_out.at[:, origin, column] if part is None else f_out.at[pl.ds(2 * part, 2), origin, column]

    def send_f(origin, d, slot, column, part, forward_to):
        ref = f_part(column, origin, part)
        go(remote(ref, ref, fx_send.at[d, slot], fx_recv.at[d, slot], device(forward_to, y, z, core)))

    def wait_f(origin, d, slot, column, part):
        ref = f_part(column, origin, part)
        remote(ref, ref, fx_send.at[d, slot], fx_recv.at[d, slot], device(right, y, z, core)).wait_recv()

    def u_first(d):
        origin = wrap(z - d, NZ)
        ref = u_out.at[y, origin]
        arrived = remote(ref, ref, uz_send.at[0, 0], uz_recv.at[d], device(x, y, z, core))
        if d == 0:
            mine = z % NC == core

            @pl.when(mine)
            def _():
                pltpu.make_async_copy(ref, ref, local_sem.at[1]).wait()

            @pl.when(jnp.logical_not(mine))
            def _():
                arrived.wait_recv()
        else:
            arrived.wait_recv()
        send_u(origin, d, 0, y, None, up)
        send_u(origin, d, 1, y, None, down)

    def u_second(d):
        origin = wrap(z - d, NZ)
        wait_u(origin, d, 0, down, None)
        send_u(origin, d, 2, down, 0, up)
        wait_u(origin, d, 1, up, None)
        send_u(origin, d, 3, up, 1, down)

    def u_last(d):
        origin = wrap(z - d, NZ)
        far = wrap(y + 2, NY)
        wait_u(origin, d, 2, far, 0)
        wait_u(origin, d, 3, far, 1)

    def f_first(d):
        origin = wrap(z - d, NZ)
        ref = f_out.at[:, origin, x]
        if d == 0:
            f_keep.wait()
        else:
            remote(ref, ref, fz_send.at[d], fz_recv.at[d], device(x, y, z, core)).wait_recv()
        send_f(origin, d, 0, x, None, right)
        send_f(origin, d, 1, x, None, left)

    def f_second(d):
        origin = wrap(z - d, NZ)
        wait_f(origin, d, 0, left, None)
        send_f(origin, d, 2, left, 0, right)
        wait_f(origin, d, 1, right, None)
        send_f(origin, d, 3, right, 1, left)

    def f_last(d):
        origin = wrap(z - d, NZ)
        far = wrap(x + 2, NX)
        wait_f(origin, d, 2, far, 0)
        wait_f(origin, d, 3, far, 1)

    f_first(0)
    for step in range(NZ + 3):
        if step < NZ:
            u_first(Z_ORDER[step])
        if 1 <= step <= NZ - 1:
            f_first(Z_ORDER[step])
        if 1 <= step <= NZ:
            u_second(Z_ORDER[step - 1])
        if 2 <= step <= NZ + 1:
            f_second(Z_ORDER[step - 2])
        if 2 <= step <= NZ + 1:
            u_last(Z_ORDER[step - 2])
        if 3 <= step <= NZ + 2:
            f_last(Z_ORDER[step - 3])

    @pl.when(swapped)
    def _():
        for copy in stat_copies:
            copy.wait()

    @pl.when(jnp.logical_not(swapped))
    def _():
        stat_keep.wait()

    for copy in sends:
        copy.wait_send()
    for c in range(NC):
        @pl.when(jnp.logical_not(here & (core == c)))
        def _():
            remote(
                u_tile(c, z), u_out.at[y, z], uz_send.at[0, c], uz_recv.at[0], device(x, y, z, 1 - core)
            ).wait_send()


def gather_inputs(features, upstream, stats):
    dma = pltpu.SemaphoreType.DMA
    f_all, u_all, stat = pl.pallas_call(
        gather_kernel,
        out_shape=(
            jax.ShapeDtypeStruct((NY, NZ, NX, 16, BLOCK), jnp.bfloat16),
            jax.ShapeDtypeStruct((NY, NZ, 64, BLOCK), jnp.bfloat16),
            jax.ShapeDtypeStruct((BLOCK, BLOCK), jnp.float32),
        ),
        in_specs=[pl.BlockSpec(memory_space=pl.ANY)] * 3,
        out_specs=(pl.BlockSpec(memory_space=pl.ANY),) * 3,
        scratch_shapes=[
            pltpu.VMEM((NY, 16, 1024), jnp.bfloat16),
            dma((4,)), dma((4,)),
            dma((NY,)), dma((NY,)), dma((NZ,)), dma((NZ,)), dma((NZ, 4)), dma((NZ, 4)),
            dma((4, NC)), dma((NZ,)), dma((NZ, 4)), dma((NZ, 4)), dma((4,)),
        ],
        compiler_params=pltpu.CompilerParams(collective_id=0, has_side_effects=True),
    )(features, upstream, stats)
    return f_all.reshape(-1, BLOCK), u_all.reshape(-1, BLOCK), stat


def spread_plan():
    rows = (ROWS_A, ROWS_B)
    first, second = (0, 1), (1, 0)
    sizes = (NY, NZ)

    def onward(part):
        kind, offsets, half = part
        out = []
        for level, axis in enumerate((first, second)[kind]):
            far = sizes[axis] // 2
            offset = offsets[axis]
            later = (first, second)[kind][level + 1 :]
            if any(offsets[other] != 0 for other in later):
                continue
            for sign in (1, -1):
                if offset * sign > 0 or abs(offset) == far:
                    continue
                moved = list(offsets)
                moved[axis] = offset - sign
                if abs(moved[axis]) == far:
                    moved[axis] = far
                    out.append((axis, sign, (kind, tuple(moved), 0 if sign == 1 else 1)))
                else:
                    out.append((axis, sign, (kind, tuple(moved), None)))
        return out

    return rows, onward


def spread_schedule():
    rows, onward = spread_plan()
    link_free = {}
    events = []
    pending = []
    halves = {}

    def launch(time, part):
        sends = []
        for axis, sign, moved in onward(part):
            count = rows[moved[0]] // (1 if moved[2] is None else 2)
            begin = max(time, link_free.get((axis, sign), 0.0))
            done = begin + count * BLOCK * 2 * 2 / 100e3
            link_free[(axis, sign)] = done
            pending.append((done + 1.0, len(pending), moved))
            sends.append((axis, sign, moved))
        return sends

    start = [launch(0.0, (kind, (0, 0), None)) for kind in (1, 0)]
    while pending:
        pending.sort()
        time, _, part = pending.pop(0)
        kind, offsets, half = part
        if half is not None:
            halves[(kind, offsets)] = halves.get((kind, offsets), 0) + 1
            if halves[(kind, offsets)] == 2:
                events.append((part, launch(time, (kind, offsets, None))))
            else:
                events.append((part, []))
        else:
            events.append((part, launch(time, part)))
    return [send for group in start for send in group], events


def split(value):
    high = value.astype(jnp.bfloat16)
    return high, (value - high.astype(jnp.float32)).astype(jnp.bfloat16)


def product(first, second):
    dot = functools.partial(jnp.dot, preferred_element_type=jnp.float32)
    return dot(first[0], second[0]) + (dot(first[0], second[1]) + dot(first[1], second[0]))


def newton_root(stat, iterate, coupled):
    def advance(now, now_parts):
        change = split((product(now_parts, now_parts) - 10.0 * now) * (1 / 16))
        once = (25 / 16) * now + product(change, now_parts)
        return (25 / 16) * once + product(change, split(once))

    start = stat[...]
    factor = 2.5 / jnp.sqrt(jnp.sum(start * start, keepdims=True))
    start = start * factor
    shape = (BLOCK, BLOCK)
    diagonal = lax.broadcasted_iota(jnp.int32, shape, 0) == lax.broadcasted_iota(jnp.int32, shape, 1)
    iterate[...] = jnp.sqrt(jnp.sqrt(factor)) * (jnp.where(diagonal, 1.25, 0.0) - 0.25 * start)
    coupled[...] = advance(start, split(start))

    def body(_, carry):
        now, root = coupled[...], iterate[...]
        now_parts = split(now)
        iterate[...] = 1.25 * root - 0.25 * product(split(root), now_parts)
        coupled[...] = advance(now, now_parts)
        return carry

    lax.fori_loop(0, ITERS - 2, body, 0)
    root = iterate[...]
    iterate[...] = 1.25 * root - 0.25 * product(split(root), split(coupled[...]))


def step_kernel(
    partial, stats, accum, out, new_stat, new_accum,
    partial_other, block, stat, iterate, coupled, root_other, pieces, precond, sums,
    other_block, shard, mp_sums, y_sums, z_sums, mp_total, y_total,
    core_sem, piece_send, piece_recv, stat_sem, root_sem,
    mp_send, mp_recv, ys_send, ys_recv, zs_send, zs_recv, swap_sem, send_sem, recv_sem, local_sem,
):
    x, y, z, core = place()
    mp = x * NC + core
    mp_peers = [(y * NZ + z, wrap(mp + j, NX * NC)) for j in range(1, NX * NC)]
    y_peers = [device(x, wrap(y + j, NY), z, core) for j in range(1, NY)]
    z_peers = [device(x, y, wrap(z + j, NZ), core) for j in range(1, NZ)]
    swapped = z % NC != core
    straight = jnp.logical_not(swapped)
    left_side = core == 0
    right_side = core == 1
    other_core = device(x, y, z, 1 - core)
    swap_peer = device(x, y, z + 1 - 2 * (z % NC), 1 - core)
    greet(mp_peers + y_peers + z_peers + [swap_peer])

    exchange = remote(partial, partial_other, core_sem.at[0], core_sem.at[1], other_core)
    exchange.start()
    shape = (BLOCK, BLOCK)
    below = lax.broadcasted_iota(jnp.int32, shape, 0) // 128 > lax.broadcasted_iota(jnp.int32, shape, 1) // 128
    kept = stats[...]
    stat[...] = jnp.where(below & swapped, kept.T, kept)
    exchange.wait()
    both = partial[...] + partial_other[...]
    block[...] = both

    member, quad, column = z % 4, z // 4 * 4, (z // 2) % 2

    def piece_rows(row):
        return block.at[pl.ds(pl.multiple_of(row * 128, 128), 128), :]

    piece_copies = []
    for j in range(1, 4):
        row = wrap(member + j, 4)
        piece_copies.append(
            remote(
                piece_rows(row), pieces.at[column], piece_send.at[j], piece_recv.at[column],
                device(x, y, quad + row, core),
            )
        )
    piece_keep = pltpu.make_async_copy(piece_rows(member), pieces.at[column], piece_send.at[0])

    @pl.when(straight)
    def _():
        for copy in piece_copies:
            copy.start()
        piece_keep.start()

    turned = both.T
    first = jnp.where(left_side, both, turned)
    second = jnp.where(left_side, turned, both)
    stat[...] = stat[...] + product(split(first), split(second))
    stat_back = remote(stat, new_stat, stat_sem.at[0], stat_sem.at[1], swap_peer)

    @pl.when(swapped)
    def _():
        stat_back.start()

    @pl.when(straight)
    def _():
        new_stat[...] = stat[...]

    newton_root(stat, iterate, coupled)

    lower = pl.ds(HALF, HALF)
    upper = pl.ds(0, HALF)
    left_sent = remote(
        iterate.at[lower, :], root_other.at[upper, :], root_sem.at[0], root_sem.at[1], other_core
    )
    right_sent = remote(iterate, root_other, root_sem.at[0], root_sem.at[1], other_core)

    @pl.when(left_side)
    def _():
        left_sent.start()

    @pl.when(right_side)
    def _():
        right_sent.start()

    for c in range(2):
        origin = 2 * c + core

        @pl.when(origin == member)
        def _():
            piece_keep.wait()

        @pl.when(origin != member)
        def _():
            remote(pieces.at[c], pieces.at[c], piece_send.at[1], piece_recv.at[c], other_core).wait_recv()

    adagrad_total = jnp.zeros((1, 1), jnp.float32)
    for c in range(2):
        columns = slice(c * BLOCK, (c + 1) * BLOCK)
        squares = pieces[c] * pieces[c]
        grown = accum[:, columns] + squares
        new_accum[:, columns] = grown
        adagrad_total = adagrad_total + jnp.sum(squares / grown, keepdims=True)

    @pl.when(left_side)
    def _():
        rows = product(split(iterate[upper, :]), split(block[...]))
        left_sent.wait_send()
        right_sent.wait_recv()
        precond[...] = product(split(rows), split(root_other[...]))

    @pl.when(right_side)
    def _():
        columns = product(split(block[...]), split(iterate[...]))
        right_sent.wait_send()
        left_sent.wait_recv()
        precond[...] = product(split(root_other[upper, :]), split(columns))

    precond_total = jnp.sum(precond[...] * precond[...], keepdims=True)
    sums[...] = jnp.where(
        lax.broadcasted_iota(jnp.int32, sums.shape, 0) == 0, adagrad_total, precond_total
    )

    swap = remote(precond, other_block, swap_sem.at[0], swap_sem.at[1], swap_peer)

    @pl.when(swapped)
    def _():
        swap.start()

    def reduce_over(peers, source, slots, sends, recvs):
        copies = [
            remote(source, slots.at[j], sends.at[j], recvs.at[j], peer) for j, peer in enumerate(peers)
        ]
        for copy in copies:
            copy.start()
        total = source[...]
        for j, copy in enumerate(copies):
            copy.wait_recv()
            total = total + slots[j]
        return total, copies

    total, sent_mp = reduce_over(mp_peers, sums, mp_sums, mp_send, mp_recv)
    mp_total[...] = total
    total, sent_y = reduce_over(y_peers, mp_total, y_sums, ys_send, ys_recv)
    y_total[...] = total
    total, sent_z = reduce_over(z_peers, y_total, z_sums, zs_send, zs_recv)
    scale = jnp.sqrt(total[0:1, 0:1] / (total[1:2, 0:1] + 1e-12))

    @pl.when(swapped)
    def _():
        swap.wait()
        shard[...] = (other_block[...] * scale).astype(jnp.bfloat16)

    @pl.when(straight)
    def _():
        shard[...] = (precond[...] * scale).astype(jnp.bfloat16)

    first_row, row_count = (0, ROWS_A), (ROWS_A, ROWS_B)

    def region(part):
        kind, (a, b), half = part
        row, depth = wrap(y + a, NY), wrap(z + b, NZ)
        count = row_count[kind]
        begin = row * 1024 + depth // 4 * BLOCK + depth % 2 * HALF + first_row[kind]
        if half is not None:
            count //= 2
            begin = begin + half * count
        column = pl.multiple_of((depth // 2) % 2 * BLOCK, BLOCK)
        return out.at[pl.ds(pl.multiple_of(begin, 16), count), pl.ds(column, BLOCK)]

    start, events = spread_schedule()
    keys = [part for part, _ in events]
    sent = []

    def send(axis, sign, moved):
        kind, offsets, half = moved
        mine = list(offsets)
        mine[axis] += sign
        if offsets[axis] == (NY, NZ)[axis] // 2:
            mine[axis] = sign * offsets[axis] * -1 + sign
        mine = tuple(mine)
        here = region((kind, mine, half))
        if mine == (0, 0):
            count = row_count[kind] // (1 if half is None else 2)
            source = shard.at[pl.ds(first_row[kind] + (half or 0) * count, count), :]
        else:
            source = here
        target = (
            device(x, wrap(y + sign, NY), z, core) if axis == 0 else device(x, y, wrap(z + sign, NZ), core)
        )
        index = keys.index(moved)
        copy = remote(source, here, send_sem.at[index], recv_sem.at[index], target)
        copy.start()
        sent.append(copy)

    for one in start:
        send(*one)
    whole = pltpu.make_async_copy(
        shard,
        out.at[
            pl.ds(pl.multiple_of(y * 1024 + z // 4 * BLOCK + z % 2 * HALF, HALF), HALF),
            pl.ds(pl.multiple_of((z // 2) % 2 * BLOCK, BLOCK), BLOCK),
        ],
        local_sem.at[0],
    )
    whole.start()
    for index, (part, onward) in enumerate(events):
        here = region(part)
        remote(here, here, send_sem.at[index], recv_sem.at[index], swap_peer).wait_recv()
        for one in onward:
            send(*one)
    for copy in sent + sent_mp + sent_y + sent_z:
        copy.wait_send()
    whole.wait()

    @pl.when(swapped)
    def _():
        stat_back.wait()

    @pl.when(straight)
    def _():
        for copy in piece_copies:
            copy.wait_send()


def take_step(partial, stats, accum):
    dma = pltpu.SemaphoreType.DMA
    tile = (8, 128)
    count = len(spread_schedule()[1])
    square = pltpu.VMEM((BLOCK, BLOCK), jnp.float32)
    vmem = pl.BlockSpec(memory_space=pltpu.VMEM)
    return pl.pallas_call(
        step_kernel,
        out_shape=(
            jax.ShapeDtypeStruct((NY * NZ * 128, 1024), jnp.bfloat16),
            jax.ShapeDtypeStruct((BLOCK, BLOCK), jnp.float32),
            jax.ShapeDtypeStruct(accum.shape, jnp.float32),
        ),
        in_specs=[vmem] * 3,
        out_specs=(pl.BlockSpec(memory_space=pl.ANY), vmem, vmem),
        scratch_shapes=[
            square, square, square, square, square, square,
            pltpu.VMEM((2, 128, BLOCK), jnp.float32),
            pltpu.VMEM((HALF, BLOCK), jnp.float32),
            pltpu.VMEM(tile, jnp.float32),
            pltpu.VMEM((HALF, BLOCK), jnp.float32),
            pltpu.VMEM((HALF, BLOCK), jnp.bfloat16),
            pltpu.VMEM((NX * NC, *tile), jnp.float32),
            pltpu.VMEM((NY, *tile), jnp.float32),
            pltpu.VMEM((NZ, *tile), jnp.float32),
            pltpu.VMEM(tile, jnp.float32),
            pltpu.VMEM(tile, jnp.float32),
            dma((2,)), dma((4,)), dma((2,)), dma((2,)), dma((2,)),
            dma((NX * NC,)), dma((NX * NC,)), dma((NY,)), dma((NY,)), dma((NZ,)), dma((NZ,)),
            dma((2,)), dma((count,)), dma((count,)), dma((1,)),
        ],
        compiler_params=pltpu.CompilerParams(
            collective_id=1, has_side_effects=True, vmem_limit_bytes=48 * 2**20
        ),
    )(partial, stats, accum)


def shards(features, upstream, stats, accum):
    f_all, u_all, stat = gather_inputs(features, upstream, stats[0, 0])
    partial = lax.dot_general(
        f_all, u_all, (((0,), (0,)), ((), ())), preferred_element_type=jnp.float32
    )
    update, new_stat, new_accum = take_step(partial, stat, accum)
    return (new_stat[None, None], new_accum, update)


def solution(mesh):
    placed = (P("dp", None), P("dp", "mp"), P("dp", "mp", None, None), P("dp", "mp"))
    return jax.shard_map(
        shards,
        mesh=mesh,
        in_specs=placed,
        out_specs=(P("dp", "mp", None, None), P("dp", "mp"), P(None, "mp")),
        check_vma=False,
    )
```

```python
import functools

import jax
import jax.numpy as jnp
from jax import lax
from jax.experimental import pallas as pl
from jax.experimental.pallas import tpu as pltpu
from jax.sharding import PartitionSpec as P

ITERS = 6
NX, NY, NZ, NC = 4, 4, 8, 2
MESH = pl.DeviceIdType.MESH
BLOCK = 512
HALF = BLOCK // 2
ROWS_A = 96
ROWS_B = HALF - ROWS_A


def place():
    dp, mp = lax.axis_index("dp"), lax.axis_index("mp")
    return mp // NC, dp // NZ, dp % NZ, mp % NC


def device(x, y, z, core):
    return (y * NZ + z, x * NC + core)


def wrap(value, size):
    return lax.rem(value + size, size)


def greet(partners):
    barrier = pltpu.get_barrier_semaphore()
    for partner in partners:
        pl.semaphore_signal(barrier, inc=1, device_id=partner, device_id_type=MESH)
    pl.semaphore_wait(barrier, len(partners))


def remote(src, dst, send_sem, recv_sem, target):
    return pltpu.make_async_remote_copy(
        src_ref=src,
        dst_ref=dst,
        send_sem=send_sem,
        recv_sem=recv_sem,
        device_id=target,
        device_id_type=MESH,
    )


def gather_block(
    features, upstream, partial, f_all, u_all, f_y,
    fy_send, fy_recv, fz_send, fz_recv, fx_send, fx_recv,
    uz_send, uz_recv, uy_send, uy_recv, keep_sem, send_stats,
):
    x, y, z, core = place()
    up, down, far_y = wrap(y + 1, NY), wrap(y - 1, NY), wrap(y + 2, NY)
    right, left, far_x = wrap(x + 1, NX), wrap(x - 1, NX), wrap(x + 2, NX)
    here = device(x, y, z, core)
    sends = []

    def go(copy):
        copy.start()
        sends.append(copy)

    def origin(d):
        return wrap(z - d, NZ)

    my_tokens = pl.ds(pl.multiple_of(64 * core + 16 * x, 16), 16)

    def f_cols(row):
        return features.at[my_tokens, pl.ds(pl.multiple_of(row * 1024, 1024), 1024)]

    def fy_start():
        for a in (2, 1, 3):
            row = wrap(y + a, NY)
            go(remote(f_cols(row), f_y.at[y], fy_send.at[a], fy_recv.at[a], device(x, row, z, core)))

    f_own = pltpu.make_async_copy(f_cols(y), f_y.at[y], keep_sem.at[0])

    def fy_wait():
        f_own.wait()
        for a in (1, 3, 2):
            into = f_y.at[wrap(y - a, NY)]
            remote(into, into, fy_send.at[a], fy_recv.at[a], here).wait_recv()

    def f_half(row):
        return f_y.at[:, :, pl.ds(pl.multiple_of(row // 4 * BLOCK, BLOCK), BLOCK)]

    f_keep = pltpu.make_async_copy(f_half(z), f_all.at[z, :, x], keep_sem.at[1])

    def fz_start(*distances):
        for d in distances:
            row = wrap(z + d, NZ)
            go(
                remote(
                    f_half(row), f_all.at[z, :, x], fz_send.at[d], fz_recv.at[d], device(x, y, row, core)
                )
            )

    parity = wrap(core - z % NC, NC)
    on_chip = parity == 0

    def u_tile(token_half, row):
        column = pl.multiple_of((row // 2) % 2 * BLOCK, BLOCK)
        return upstream.at[pl.ds(64 * token_half, 64), pl.ds(column, BLOCK)]

    u_keep = pltpu.make_async_copy(u_tile(core, z), u_all.at[z, y], keep_sem.at[2])

    def u_remote(j, c):
        d = 2 * j + parity
        row = wrap(z + d, NZ)
        return remote(
            u_tile(c, row), u_all.at[z, y], uz_send.at[j, c], uz_recv.at[d], device(x, y, row, c)
        )

    def uz_start(*steps):
        for j in steps:
            for c in range(NC):
                copy = u_remote(j, c)
                if j == 0:
                    pl.when(jnp.logical_not(on_chip & (core == c)))(copy.start)
                else:
                    go(copy)

    def uz_finish():
        for c in range(NC):
            pl.when(jnp.logical_not(on_chip & (core == c)))(u_remote(0, c).wait_send)

    def u_part(d, row, part):
        ref = u_all.at[origin(d), row]
        return ref if part is None else ref.at[pl.ds(32 * part, 32), :]

    def u_copy(d, slot, row, part, target):
        ref = u_part(d, row, part)
        return remote(ref, ref, uy_send.at[d, slot], uy_recv.at[d, slot], device(x, target, z, core))

    def f_part(d, column, part):
        if part is None:
            return f_all.at[origin(d), :, column]
        return f_all.at[origin(d), pl.ds(2 * part, 2), column]

    def f_copy(d, slot, column, part, target):
        ref = f_part(d, column, part)
        return remote(ref, ref, fx_send.at[d, slot], fx_recv.at[d, slot], device(target, y, z, core))

    def u1(d):
        ref = u_all.at[origin(d), y]
        arrived = remote(ref, ref, uz_send.at[0, 0], uz_recv.at[d], here)
        if d == 0:
            pl.when(on_chip)(u_keep.wait)
            pl.when(jnp.logical_not(on_chip))(arrived.wait_recv)
        else:
            arrived.wait_recv()
        go(u_copy(d, 0, y, None, up))
        go(u_copy(d, 1, y, None, down))

    def u2(d):
        u_copy(d, 0, down, None, up).wait_recv()
        go(u_copy(d, 2, down, 0, up))
        u_copy(d, 1, up, None, down).wait_recv()
        go(u_copy(d, 3, up, 1, down))

    def f1(d):
        ref = f_all.at[origin(d), :, x]
        if d == 0:
            f_keep.wait()
        else:
            remote(ref, ref, fz_send.at[d], fz_recv.at[d], here).wait_recv()
        go(f_copy(d, 0, x, None, right))
        go(f_copy(d, 1, x, None, left))

    def f2(d):
        f_copy(d, 0, left, None, right).wait_recv()
        go(f_copy(d, 2, left, 0, right))
        f_copy(d, 1, right, None, left).wait_recv()
        go(f_copy(d, 3, right, 1, left))

    def add(d):
        for part in range(2):
            u_copy(d, 2 + part, far_y, part, up).wait_recv()
            f_copy(d, 2 + part, far_x, part, right).wait_recv()
        term = lax.dot_general(
            f_all[origin(d)].reshape(256, BLOCK),
            u_all[origin(d)].reshape(256, BLOCK),
            (((0,), (0,)), ((), ())),
            preferred_element_type=jnp.float32,
        )
        partial[...] = term if d == 0 else partial[...] + term

    fy_start()
    f_own.start()
    uz_start(0, 3)
    pl.when(on_chip)(u_keep.start)
    fy_wait()
    fz_start(1, 7)
    f_keep.start()
    u1(0)
    f1(0)
    for d in (1, 7):
        u1(d)
    for d in (1, 7):
        f1(d)
    fz_start(2, 6)
    u1(6)
    uz_start(1, 2)
    for d in (0, 1, 7):
        u2(d)
        f2(d)
    for d in (2, 6):
        f1(d)
    fz_start(3, 5)
    u2(6)
    f2(2)
    for d in (2, 3, 5, 4):
        u1(d)
    fz_start(4)
    send_stats()
    add(0)
    f2(6)
    u2(2)
    u2(3)
    add(1)
    f1(3)
    f1(5)
    u2(5)
    u2(4)
    add(7)
    f2(3)
    f2(5)
    f1(4)
    add(6)
    add(2)
    f2(4)
    add(3)
    add(5)
    add(4)
    return sends, uz_finish


def spread_plan():
    rows = (ROWS_A, ROWS_B)
    first, second = (0, 1), (1, 0)
    sizes = (NY, NZ)

    def onward(part):
        kind, offsets, half = part
        out = []
        for level, axis in enumerate((first, second)[kind]):
            far = sizes[axis] // 2
            offset = offsets[axis]
            later = (first, second)[kind][level + 1 :]
            if any(offsets[other] != 0 for other in later):
                continue
            for sign in (1, -1):
                if offset * sign > 0 or abs(offset) == far:
                    continue
                moved = list(offsets)
                moved[axis] = offset - sign
                if abs(moved[axis]) == far:
                    moved[axis] = far
                    out.append((axis, sign, (kind, tuple(moved), 0 if sign == 1 else 1)))
                else:
                    out.append((axis, sign, (kind, tuple(moved), None)))
        return out

    return rows, onward


def spread_schedule():
    rows, onward = spread_plan()
    link_free = {}
    events = []
    pending = []
    halves = {}

    def launch(time, part):
        sends = []
        for axis, sign, moved in onward(part):
            count = rows[moved[0]] // (1 if moved[2] is None else 2)
            begin = max(time, link_free.get((axis, sign), 0.0))
            done = begin + count * BLOCK * 2 * 2 / 100e3
            link_free[(axis, sign)] = done
            pending.append((done + 1.0, len(pending), moved))
            sends.append((axis, sign, moved))
        return sends

    start = [launch(0.0, (kind, (0, 0), None)) for kind in (1, 0)]
    while pending:
        pending.sort()
        time, _, part = pending.pop(0)
        kind, offsets, half = part
        if half is not None:
            halves[(kind, offsets)] = halves.get((kind, offsets), 0) + 1
            if halves[(kind, offsets)] == 2:
                events.append((part, launch(time, (kind, offsets, None))))
            else:
                events.append((part, []))
        else:
            events.append((part, launch(time, part)))
    return [send for group in start for send in group], events


def split(value):
    high = value.astype(jnp.bfloat16)
    return high, (value - high.astype(jnp.float32)).astype(jnp.bfloat16)


def product(first, second):
    dot = functools.partial(jnp.dot, preferred_element_type=jnp.float32)
    return dot(first[0], second[0]) + (dot(first[0], second[1]) + dot(first[1], second[0]))


def newton_root(stat, iterate, coupled):
    def advance(now, now_parts):
        change = split((product(now_parts, now_parts) - 10.0 * now) * (1 / 16))
        once = (25 / 16) * now + product(change, now_parts)
        return (25 / 16) * once + product(change, split(once))

    start = stat[...]
    factor = 2.5 / jnp.sqrt(jnp.sum(start * start, keepdims=True))
    start = start * factor
    shape = (BLOCK, BLOCK)
    diagonal = lax.broadcasted_iota(jnp.int32, shape, 0) == lax.broadcasted_iota(jnp.int32, shape, 1)
    iterate[...] = jnp.sqrt(jnp.sqrt(factor)) * (jnp.where(diagonal, 1.25, 0.0) - 0.25 * start)
    coupled[...] = advance(start, split(start))

    def body(_, carry):
        now, root = coupled[...], iterate[...]
        now_parts = split(now)
        iterate[...] = 1.25 * root - 0.25 * product(split(root), now_parts)
        coupled[...] = advance(now, now_parts)
        return carry

    lax.fori_loop(0, ITERS - 2, body, 0)
    root = iterate[...]
    iterate[...] = 1.25 * root - 0.25 * product(split(root), split(coupled[...]))


def step_kernel(
    features, upstream, stats, accum, out, new_stat, new_accum,
    f_all, u_all, f_y, accum_here, stat_other, partial, partial_other, block, stat, iterate, coupled, root_other, pieces, precond, sums,
    other_block, shard, mp_sums, y_sums, z_sums, mp_total, y_total,
    fy_send, fy_recv, fz_send, fz_recv, fx_send, fx_recv, uz_send, uz_recv, uy_send, uy_recv, keep_sem,
    load_sem, stats_send, stats_recv, core_sem, piece_send, piece_recv, stat_sem, root_sem,
    mp_send, mp_recv, ys_send, ys_recv, zs_send, zs_recv, swap_sem, send_sem, recv_sem, local_sem,
):
    x, y, z, core = place()
    mp = x * NC + core
    mp_peers = [(y * NZ + z, wrap(mp + j, NX * NC)) for j in range(1, NX * NC)]
    y_peers = [device(x, wrap(y + j, NY), z, core) for j in range(1, NY)]
    z_peers = [device(x, y, wrap(z + j, NZ), core) for j in range(1, NZ)]
    swapped = z % NC != core
    straight = jnp.logical_not(swapped)
    left_side = core == 0
    right_side = core == 1
    other_core = device(x, y, z, 1 - core)
    swap_peer = device(x, y, z + 1 - 2 * (z % NC), 1 - core)
    across = [device(x, y, wrap(z + j, NZ), 1 - core) for j in range(1, NZ)]
    greet(mp_peers + y_peers + z_peers + across)
    accum_load = pltpu.make_async_copy(accum, accum_here, load_sem.at[0])
    stat_load = pltpu.make_async_copy(stats, stat, load_sem.at[1])
    accum_load.start()
    pl.when(straight)(stat_load.start)

    stat_copies = []
    for i in range(4):
        at = pl.ds(128 * i, 128), pl.ds(128 * i, BLOCK - 128 * i)
        stat_copies.append(
            remote(stats.at[at], stat_other.at[at], stats_send.at[i], stats_recv.at[i], swap_peer)
        )

    def send_stats():
        for copy in stat_copies:
            pl.when(swapped)(copy.start)

    gather_sends, gather_finish = gather_block(
        features, upstream, partial, f_all, u_all, f_y,
        fy_send, fy_recv, fz_send, fz_recv, fx_send, fx_recv,
        uz_send, uz_recv, uy_send, uy_recv, keep_sem, send_stats,
    )

    exchange = remote(partial, partial_other, core_sem.at[0], core_sem.at[1], other_core)
    exchange.start()

    @pl.when(swapped)
    def _():
        for copy in stat_copies:
            copy.wait()
        for i in range(1, 4):
            for j in range(i):
                stat_other[128 * i : 128 * i + 128, 128 * j : 128 * j + 128] = stat_other[
                    128 * j : 128 * j + 128, 128 * i : 128 * i + 128
                ].T
        stat[...] = stat_other[...]

    @pl.when(straight)
    def _():
        stat_load.wait()

    exchange.wait()
    both = partial[...] + partial_other[...]
    block[...] = both

    member, quad, column = z % 4, z // 4 * 4, (z // 2) % 2

    def piece_rows(row):
        return block.at[pl.ds(pl.multiple_of(row * 128, 128), 128), :]

    piece_copies = []
    for j in range(1, 4):
        row = wrap(member + j, 4)
        piece_copies.append(
            remote(
                piece_rows(row), pieces.at[column], piece_send.at[j], piece_recv.at[column],
                device(x, y, quad + row, core),
            )
        )
    piece_keep = pltpu.make_async_copy(piece_rows(member), pieces.at[column], piece_send.at[0])

    @pl.when(straight)
    def _():
        for copy in piece_copies:
            copy.start()
        piece_keep.start()

    turned = both.T
    first = jnp.where(left_side, both, turned)
    second = jnp.where(left_side, turned, both)
    stat[...] = stat[...] + product(split(first), split(second))
    stat_back = remote(stat, new_stat, stat_sem.at[0], stat_sem.at[1], swap_peer)

    @pl.when(swapped)
    def _():
        stat_back.start()

    @pl.when(straight)
    def _():
        new_stat[...] = stat[...]

    newton_root(stat, iterate, coupled)

    lower = pl.ds(HALF, HALF)
    upper = pl.ds(0, HALF)
    left_sent = remote(
        iterate.at[lower, :], root_other.at[upper, :], root_sem.at[0], root_sem.at[1], other_core
    )
    right_sent = remote(iterate, root_other, root_sem.at[0], root_sem.at[1], other_core)

    @pl.when(left_side)
    def _():
        left_sent.start()

    @pl.when(right_side)
    def _():
        right_sent.start()

    for c in range(2):
        origin = 2 * c + core

        @pl.when(origin == member)
        def _():
            piece_keep.wait()

        @pl.when(origin != member)
        def _():
            remote(pieces.at[c], pieces.at[c], piece_send.at[1], piece_recv.at[c], other_core).wait_recv()

    accum_load.wait()
    adagrad_total = jnp.zeros((1, 1), jnp.float32)
    for c in range(2):
        columns = slice(c * BLOCK, (c + 1) * BLOCK)
        squares = pieces[c] * pieces[c]
        grown = accum_here[:, columns] + squares
        new_accum[:, columns] = grown
        adagrad_total = adagrad_total + jnp.sum(squares / grown, keepdims=True)

    @pl.when(left_side)
    def _():
        rows = product(split(iterate[upper, :]), split(block[...]))
        left_sent.wait_send()
        right_sent.wait_recv()
        precond[...] = product(split(rows), split(root_other[...]))

    @pl.when(right_side)
    def _():
        columns = product(split(block[...]), split(iterate[...]))
        right_sent.wait_send()
        left_sent.wait_recv()
        precond[...] = product(split(root_other[upper, :]), split(columns))

    precond_total = jnp.sum(precond[...] * precond[...], keepdims=True)
    sums[...] = jnp.where(
        lax.broadcasted_iota(jnp.int32, sums.shape, 0) == 0, adagrad_total, precond_total
    )

    swap = remote(precond, other_block, swap_sem.at[0], swap_sem.at[1], swap_peer)

    @pl.when(swapped)
    def _():
        swap.start()

    def reduce_over(peers, source, slots, sends, recvs):
        copies = [
            remote(source, slots.at[j], sends.at[j], recvs.at[j], peer) for j, peer in enumerate(peers)
        ]
        for copy in copies:
            copy.start()
        total = source[...]
        for j, copy in enumerate(copies):
            copy.wait_recv()
            total = total + slots[j]
        return total, copies

    total, sent_mp = reduce_over(mp_peers, sums, mp_sums, mp_send, mp_recv)
    mp_total[...] = total
    total, sent_y = reduce_over(y_peers, mp_total, y_sums, ys_send, ys_recv)
    y_total[...] = total
    total, sent_z = reduce_over(z_peers, y_total, z_sums, zs_send, zs_recv)
    scale = jnp.sqrt(total[0:1, 0:1] / (total[1:2, 0:1] + 1e-12))

    @pl.when(swapped)
    def _():
        swap.wait()
        shard[...] = (other_block[...] * scale).astype(jnp.bfloat16)

    @pl.when(straight)
    def _():
        shard[...] = (precond[...] * scale).astype(jnp.bfloat16)

    first_row, row_count = (0, ROWS_A), (ROWS_A, ROWS_B)

    def region(part):
        kind, (a, b), half = part
        row, depth = wrap(y + a, NY), wrap(z + b, NZ)
        count = row_count[kind]
        begin = row * 1024 + depth // 4 * BLOCK + depth % 2 * HALF + first_row[kind]
        if half is not None:
            count //= 2
            begin = begin + half * count
        column = pl.multiple_of((depth // 2) % 2 * BLOCK, BLOCK)
        return out.at[pl.ds(pl.multiple_of(begin, 16), count), pl.ds(column, BLOCK)]

    start, events = spread_schedule()
    keys = [part for part, _ in events]
    sent = []

    def send(axis, sign, moved):
        kind, offsets, half = moved
        mine = list(offsets)
        mine[axis] += sign
        if offsets[axis] == (NY, NZ)[axis] // 2:
            mine[axis] = sign * offsets[axis] * -1 + sign
        mine = tuple(mine)
        here = region((kind, mine, half))
        if mine == (0, 0):
            count = row_count[kind] // (1 if half is None else 2)
            source = shard.at[pl.ds(first_row[kind] + (half or 0) * count, count), :]
        else:
            source = here
        target = (
            device(x, wrap(y + sign, NY), z, core) if axis == 0 else device(x, y, wrap(z + sign, NZ), core)
        )
        index = keys.index(moved)
        copy = remote(source, here, send_sem.at[index], recv_sem.at[index], target)
        copy.start()
        sent.append(copy)

    for one in start:
        send(*one)
    whole = pltpu.make_async_copy(
        shard,
        out.at[
            pl.ds(pl.multiple_of(y * 1024 + z // 4 * BLOCK + z % 2 * HALF, HALF), HALF),
            pl.ds(pl.multiple_of((z // 2) % 2 * BLOCK, BLOCK), BLOCK),
        ],
        local_sem.at[0],
    )
    whole.start()
    for index, (part, onward) in enumerate(events):
        here = region(part)
        remote(here, here, send_sem.at[index], recv_sem.at[index], swap_peer).wait_recv()
        for one in onward:
            send(*one)
    for copy in gather_sends + sent + sent_mp + sent_y + sent_z:
        copy.wait_send()
    gather_finish()
    whole.wait()

    @pl.when(swapped)
    def _():
        stat_back.wait()

    @pl.when(straight)
    def _():
        for copy in piece_copies:
            copy.wait_send()


def take_step(features, upstream, stats, accum):
    dma = pltpu.SemaphoreType.DMA
    tile = (8, 128)
    count = len(spread_schedule()[1])
    square = pltpu.VMEM((BLOCK, BLOCK), jnp.float32)
    vmem = pl.BlockSpec(memory_space=pltpu.VMEM)
    return pl.pallas_call(
        step_kernel,
        out_shape=(
            pltpu.VMEM((NY * NZ * 128, 1024), jnp.bfloat16),
            pltpu.VMEM((BLOCK, BLOCK), jnp.float32),
            pltpu.VMEM(accum.shape, jnp.float32),
        ),
        in_specs=[pl.BlockSpec(memory_space=pltpu.HBM)] * 4,
        out_specs=(vmem, vmem, vmem),
        scratch_shapes=[
            pltpu.VMEM((NZ, NY, NX, 16, BLOCK), jnp.bfloat16),
            pltpu.VMEM((NZ, NY, 64, BLOCK), jnp.bfloat16),
            pltpu.VMEM((NY, 16, 1024), jnp.bfloat16),
            pltpu.VMEM(accum.shape, jnp.float32),
            square, square, square, square, square, square, square, square,
            pltpu.VMEM((2, 128, BLOCK), jnp.float32),
            pltpu.VMEM((HALF, BLOCK), jnp.float32),
            pltpu.VMEM(tile, jnp.float32),
            pltpu.VMEM((HALF, BLOCK), jnp.float32),
            pltpu.VMEM((HALF, BLOCK), jnp.bfloat16),
            pltpu.VMEM((NX * NC, *tile), jnp.float32),
            pltpu.VMEM((NY, *tile), jnp.float32),
            pltpu.VMEM((NZ, *tile), jnp.float32),
            pltpu.VMEM(tile, jnp.float32),
            pltpu.VMEM(tile, jnp.float32),
            dma((NY,)), dma((NY,)), dma((NZ,)), dma((NZ,)), dma((NZ, 4)), dma((NZ, 4)),
            dma((4, NC)), dma((NZ,)), dma((NZ, 4)), dma((NZ, 4)), dma((3,)),
            dma((2,)), dma((4,)), dma((4,)), dma((2,)), dma((4,)), dma((2,)), dma((2,)), dma((2,)),
            dma((NX * NC,)), dma((NX * NC,)), dma((NY,)), dma((NY,)), dma((NZ,)), dma((NZ,)),
            dma((2,)), dma((count,)), dma((count,)), dma((1,)),
        ],
        compiler_params=pltpu.CompilerParams(
            collective_id=0, has_side_effects=True, vmem_limit_bytes=50 * 2**20
        ),
    )(features, upstream, stats, accum)


def shards(features, upstream, stats, accum):
    update, new_stat, new_accum = take_step(features, upstream, stats[0, 0], accum)
    return (new_stat[None, None], new_accum, update)


def solution(mesh):
    placed = (P("dp", None), P("dp", "mp"), P("dp", "mp", None, None), P("dp", "mp"))
    return jax.shard_map(
        shards,
        mesh=mesh,
        in_specs=placed,
        out_specs=(P("dp", "mp", None, None), P("dp", "mp"), P(None, "mp")),
        check_vma=False,
    )
```

```python
import functools

import jax
import jax.numpy as jnp
from jax import lax
from jax.experimental import pallas as pl
from jax.experimental.pallas import tpu as pltpu
from jax.sharding import PartitionSpec as P

ITERS = 6
NX, NY, NZ, NC = 4, 4, 8, 2
MESH = pl.DeviceIdType.MESH
BLOCK = 512
HALF = BLOCK // 2
ROWS_A = 96
ROWS_B = HALF - ROWS_A


def place():
    dp, mp = lax.axis_index("dp"), lax.axis_index("mp")
    return mp // NC, dp // NZ, dp % NZ, mp % NC


def device(x, y, z, core):
    return (y * NZ + z, x * NC + core)


def wrap(value, size):
    return lax.rem(value + size, size)


def greet(partners):
    barrier = pltpu.get_barrier_semaphore()
    for partner in partners:
        pl.semaphore_signal(barrier, inc=1, device_id=partner, device_id_type=MESH)
    pl.semaphore_wait(barrier, len(partners))


def remote(src, dst, send_sem, recv_sem, target):
    return pltpu.make_async_remote_copy(
        src_ref=src,
        dst_ref=dst,
        send_sem=send_sem,
        recv_sem=recv_sem,
        device_id=target,
        device_id_type=MESH,
    )


def gather_block(
    features, upstream, partial, f_all, u_all, f_y,
    fy_send, fy_recv, fz_send, fz_recv, fx_send, fx_recv,
    uz_send, uz_recv, uy_send, uy_recv, keep_sem, send_stats,
):
    x, y, z, core = place()
    up, down, far_y = wrap(y + 1, NY), wrap(y - 1, NY), wrap(y + 2, NY)
    right, left, far_x = wrap(x + 1, NX), wrap(x - 1, NX), wrap(x + 2, NX)
    here = device(x, y, z, core)
    sends = []

    def go(copy):
        copy.start()
        sends.append(copy)

    def origin(d):
        return wrap(z - d, NZ)

    my_tokens = pl.ds(pl.multiple_of(64 * core + 16 * x, 16), 16)

    def f_cols(row):
        return features.at[my_tokens, pl.ds(pl.multiple_of(row * 1024, 1024), 1024)]

    def fy_start():
        for a in (2, 1, 3):
            row = wrap(y + a, NY)
            go(remote(f_cols(row), f_y.at[y], fy_send.at[a], fy_recv.at[a], device(x, row, z, core)))

    f_own = pltpu.make_async_copy(f_cols(y), f_y.at[y], keep_sem.at[0])

    def fy_wait():
        f_own.wait()
        for a in (1, 3, 2):
            into = f_y.at[wrap(y - a, NY)]
            remote(into, into, fy_send.at[a], fy_recv.at[a], here).wait_recv()

    def f_half(row):
        return f_y.at[:, :, pl.ds(pl.multiple_of(row // 4 * BLOCK, BLOCK), BLOCK)]

    f_keep = pltpu.make_async_copy(f_half(z), f_all.at[z, :, x], keep_sem.at[1])

    spot = z % 4
    maybe = []

    def go_if(condition, copy):
        pl.when(condition)(copy.start)
        maybe.append((condition, copy))

    def fz_copy(source, slot, d, row):
        into = f_all.at[wrap(row - d, NZ), :, x]
        return remote(source, into, fz_send.at[slot], fz_recv.at[d], device(x, y, row, core))

    def fz_start():
        above, below, two_up, two_down = (wrap(z + step, NZ) for step in (1, -1, 2, -2))
        go(fz_copy(f_half(above), 0, 1, above))
        go(fz_copy(f_half(below), 8, 7, below))
        go_if(spot == 1, fz_copy(f_half(two_down), 9, 6, two_down))
        go_if(spot == 2, fz_copy(f_half(two_up), 9, 2, two_up))

    def fz_pass(d):
        ref = f_all.at[origin(d), :, x]
        above, below = wrap(z + 1, NZ), wrap(z - 1, NZ)
        rising = {1: spot < 3, 2: spot < 3, 3: (spot == 1) | (spot == 2), 4: spot == 2}
        falling = {7: spot > 0, 6: spot > 0, 5: (spot == 1) | (spot == 2), 4: spot == 1}
        if d in rising:
            go_if(rising[d], fz_copy(ref, d, d + 1, above))
        if d in falling:
            go_if(falling[d], fz_copy(ref, d, d - 1, below))

    parity = wrap(core - z % NC, NC)
    on_chip = parity == 0

    def u_tile(token_half, row):
        column = pl.multiple_of((row // 2) % 2 * BLOCK, BLOCK)
        return upstream.at[pl.ds(64 * token_half, 64), pl.ds(column, BLOCK)]

    u_keep = pltpu.make_async_copy(u_tile(core, z), u_all.at[z, y], keep_sem.at[2])

    def u_remote(j, c):
        d = 2 * j + parity
        row = wrap(z + d, NZ)
        return remote(
            u_tile(c, row), u_all.at[z, y], uz_send.at[j, c], uz_recv.at[d], device(x, y, row, c)
        )

    def uz_start(*steps):
        for j in steps:
            for c in range(NC):
                copy = u_remote(j, c)
                if j == 0:
                    pl.when(jnp.logical_not(on_chip & (core == c)))(copy.start)
                else:
                    go(copy)

    def uz_finish():
        for c in range(NC):
            pl.when(jnp.logical_not(on_chip & (core == c)))(u_remote(0, c).wait_send)

    def u_part(d, row, part):
        ref = u_all.at[origin(d), row]
        return ref if part is None else ref.at[pl.ds(32 * part, 32), :]

    def u_copy(d, slot, row, part, target):
        ref = u_part(d, row, part)
        return remote(ref, ref, uy_send.at[d, slot], uy_recv.at[d, slot], device(x, target, z, core))

    def f_part(d, column, part):
        if part is None:
            return f_all.at[origin(d), :, column]
        return f_all.at[origin(d), pl.ds(2 * part, 2), column]

    def f_copy(d, slot, column, part, target):
        ref = f_part(d, column, part)
        return remote(ref, ref, fx_send.at[d, slot], fx_recv.at[d, slot], device(target, y, z, core))

    def u1(d):
        ref = u_all.at[origin(d), y]
        arrived = remote(ref, ref, uz_send.at[0, 0], uz_recv.at[d], here)
        if d == 0:
            pl.when(on_chip)(u_keep.wait)
            pl.when(jnp.logical_not(on_chip))(arrived.wait_recv)
        else:
            arrived.wait_recv()
        go(u_copy(d, 0, y, None, up))
        go(u_copy(d, 1, y, None, down))

    def u2(d):
        u_copy(d, 0, down, None, up).wait_recv()
        go(u_copy(d, 2, down, 0, up))
        u_copy(d, 1, up, None, down).wait_recv()
        go(u_copy(d, 3, up, 1, down))

    def f1(d):
        ref = f_all.at[origin(d), :, x]
        if d == 0:
            f_keep.wait()
        else:
            remote(ref, ref, fz_send.at[d], fz_recv.at[d], here).wait_recv()
            fz_pass(d)
        go(f_copy(d, 0, x, None, right))
        go(f_copy(d, 1, x, None, left))

    def f2(d):
        f_copy(d, 0, left, None, right).wait_recv()
        go(f_copy(d, 2, left, 0, right))
        f_copy(d, 1, right, None, left).wait_recv()
        go(f_copy(d, 3, right, 1, left))

    def add(d):
        for part in range(2):
            u_copy(d, 2 + part, far_y, part, up).wait_recv()
            f_copy(d, 2 + part, far_x, part, right).wait_recv()
        term = lax.dot_general(
            f_all[origin(d)].reshape(256, BLOCK),
            u_all[origin(d)].reshape(256, BLOCK),
            (((0,), (0,)), ((), ())),
            preferred_element_type=jnp.float32,
        )
        partial[...] = term if d == 0 else partial[...] + term

    fy_start()
    f_own.start()
    uz_start(0, 3)
    pl.when(on_chip)(u_keep.start)
    fy_wait()
    fz_start()
    f_keep.start()
    u1(0)
    f1(0)
    uz_start(1)
    u1(1)
    u1(7)
    f1(1)
    f1(7)
    u1(6)
    uz_start(2)
    for d in (0, 1, 7):
        u2(d)
        f2(d)
    f1(2)
    f1(6)
    u1(2)
    u1(3)
    u2(6)
    f2(2)
    f2(6)
    send_stats()
    f1(3)
    f1(5)
    u2(2)
    u2(3)
    u1(5)
    u1(4)
    add(0)
    f1(4)
    f2(3)
    f2(5)
    add(1)
    u2(5)
    u2(4)
    f2(4)
    for d in (7, 6, 2, 3, 5, 4):
        add(d)

    def finish():
        uz_finish()
        for condition, copy in maybe:
            pl.when(condition)(copy.wait_send)

    return sends, finish


def spread_plan():
    rows = (ROWS_A, ROWS_B)
    first, second = (0, 1), (1, 0)
    sizes = (NY, NZ)

    def onward(part):
        kind, offsets, half = part
        out = []
        for level, axis in enumerate((first, second)[kind]):
            far = sizes[axis] // 2
            offset = offsets[axis]
            later = (first, second)[kind][level + 1 :]
            if any(offsets[other] != 0 for other in later):
                continue
            for sign in (1, -1):
                if offset * sign > 0 or abs(offset) == far:
                    continue
                moved = list(offsets)
                moved[axis] = offset - sign
                if abs(moved[axis]) == far:
                    moved[axis] = far
                    out.append((axis, sign, (kind, tuple(moved), 0 if sign == 1 else 1)))
                else:
                    out.append((axis, sign, (kind, tuple(moved), None)))
        return out

    return rows, onward


def spread_schedule():
    rows, onward = spread_plan()
    link_free = {}
    events = []
    pending = []
    halves = {}

    def launch(time, part):
        sends = []
        for axis, sign, moved in onward(part):
            count = rows[moved[0]] // (1 if moved[2] is None else 2)
            begin = max(time, link_free.get((axis, sign), 0.0))
            done = begin + count * BLOCK * 2 * 2 / 100e3
            link_free[(axis, sign)] = done
            pending.append((done + 1.0, len(pending), moved))
            sends.append((axis, sign, moved))
        return sends

    start = [launch(0.0, (kind, (0, 0), None)) for kind in (1, 0)]
    while pending:
        pending.sort()
        time, _, part = pending.pop(0)
        kind, offsets, half = part
        if half is not None:
            halves[(kind, offsets)] = halves.get((kind, offsets), 0) + 1
            if halves[(kind, offsets)] == 2:
                events.append((part, launch(time, (kind, offsets, None))))
            else:
                events.append((part, []))
        else:
            events.append((part, launch(time, part)))
    return [send for group in start for send in group], events


def split(value):
    high = value.astype(jnp.bfloat16)
    return high, (value - high.astype(jnp.float32)).astype(jnp.bfloat16)


def product(first, second):
    dot = functools.partial(jnp.dot, preferred_element_type=jnp.float32)
    return dot(first[0], second[0]) + (dot(first[0], second[1]) + dot(first[1], second[0]))


def symmetric_product(first, second):
    left = product(first, [part[:, :HALF] for part in second])
    last = product([part[HALF:] for part in first], [part[:, HALF:] for part in second])
    return jnp.concatenate([left, jnp.concatenate([left[HALF:].T, last], 0)], 1)


def newton_root(stat, iterate, coupled):
    def advance(now, now_parts):
        change = split((symmetric_product(now_parts, now_parts) - 10.0 * now) * (1 / 16))
        once = (25 / 16) * now + symmetric_product(change, now_parts)
        return (25 / 16) * once + symmetric_product(change, split(once))

    start = stat[...]
    factor = 2.5 / jnp.sqrt(jnp.sum(start * start, keepdims=True))
    start = start * factor
    shape = (BLOCK, BLOCK)
    diagonal = lax.broadcasted_iota(jnp.int32, shape, 0) == lax.broadcasted_iota(jnp.int32, shape, 1)
    iterate[...] = jnp.sqrt(jnp.sqrt(factor)) * (jnp.where(diagonal, 1.25, 0.0) - 0.25 * start)
    coupled[...] = advance(start, split(start))

    def body(_, carry):
        now, root = coupled[...], iterate[...]
        now_parts = split(now)
        iterate[...] = 1.25 * root - 0.25 * symmetric_product(split(root), now_parts)
        coupled[...] = advance(now, now_parts)
        return carry

    lax.fori_loop(0, ITERS - 2, body, 0)
    root = iterate[...]
    iterate[...] = 1.25 * root - 0.25 * symmetric_product(split(root), split(coupled[...]))


def step_kernel(
    features, upstream, stats, accum, out, new_stat, new_accum,
    f_all, u_all, f_y, accum_here, stat_other, partial, partial_other, block, stat, iterate, coupled, root_other, pieces, precond, sums,
    other_block, shard, mp_sums, y_sums, z_sums, mp_total, y_total,
    fy_send, fy_recv, fz_send, fz_recv, fx_send, fx_recv, uz_send, uz_recv, uy_send, uy_recv, keep_sem,
    load_sem, stats_send, stats_recv, core_sem, piece_send, piece_recv, stat_sem, root_sem,
    mp_send, mp_recv, ys_send, ys_recv, zs_send, zs_recv, swap_sem, send_sem, recv_sem, local_sem,
):
    x, y, z, core = place()
    mp = x * NC + core
    mp_peers = [(y * NZ + z, wrap(mp + j, NX * NC)) for j in range(1, NX * NC)]
    y_peers = [device(x, wrap(y + j, NY), z, core) for j in range(1, NY)]
    z_peers = [device(x, y, wrap(z + j, NZ), core) for j in range(1, NZ)]
    swapped = z % NC != core
    straight = jnp.logical_not(swapped)
    left_side = core == 0
    right_side = core == 1
    other_core = device(x, y, z, 1 - core)
    swap_peer = device(x, y, z + 1 - 2 * (z % NC), 1 - core)
    across = [device(x, y, wrap(z + j, NZ), 1 - core) for j in range(1, NZ)]
    greet(mp_peers + y_peers + z_peers + across)
    accum_load = pltpu.make_async_copy(accum, accum_here, load_sem.at[0])
    stat_load = pltpu.make_async_copy(stats, stat, load_sem.at[1])
    accum_load.start()
    pl.when(straight)(stat_load.start)

    stat_copies = []
    for i in range(4):
        at = pl.ds(128 * i, 128), pl.ds(128 * i, BLOCK - 128 * i)
        stat_copies.append(
            remote(stats.at[at], stat_other.at[at], stats_send.at[i], stats_recv.at[i], swap_peer)
        )

    def send_stats():
        for copy in stat_copies:
            pl.when(swapped)(copy.start)

    gather_sends, gather_finish = gather_block(
        features, upstream, partial, f_all, u_all, f_y,
        fy_send, fy_recv, fz_send, fz_recv, fx_send, fx_recv,
        uz_send, uz_recv, uy_send, uy_recv, keep_sem, send_stats,
    )

    exchange = remote(partial, partial_other, core_sem.at[0], core_sem.at[1], other_core)
    exchange.start()

    @pl.when(swapped)
    def _():
        for copy in stat_copies:
            copy.wait()
        for i in range(1, 4):
            for j in range(i):
                stat_other[128 * i : 128 * i + 128, 128 * j : 128 * j + 128] = stat_other[
                    128 * j : 128 * j + 128, 128 * i : 128 * i + 128
                ].T
        stat[...] = stat_other[...]

    @pl.when(straight)
    def _():
        stat_load.wait()

    exchange.wait()
    both = partial[...] + partial_other[...]
    block[...] = both

    member, quad, column = z % 4, z // 4 * 4, (z // 2) % 2

    def piece_rows(row):
        return block.at[pl.ds(pl.multiple_of(row * 128, 128), 128), :]

    piece_copies = []
    for j in range(1, 4):
        row = wrap(member + j, 4)
        piece_copies.append(
            remote(
                piece_rows(row), pieces.at[column], piece_send.at[j], piece_recv.at[column],
                device(x, y, quad + row, core),
            )
        )
    piece_keep = pltpu.make_async_copy(piece_rows(member), pieces.at[column], piece_send.at[0])

    @pl.when(straight)
    def _():
        for copy in piece_copies:
            copy.start()
        piece_keep.start()

    turned = both.T
    first = jnp.where(left_side, both, turned)
    second = jnp.where(left_side, turned, both)
    stat[...] = stat[...] + symmetric_product(split(first), split(second))
    stat_back = remote(stat, new_stat, stat_sem.at[0], stat_sem.at[1], swap_peer)

    @pl.when(swapped)
    def _():
        stat_back.start()

    @pl.when(straight)
    def _():
        new_stat[...] = stat[...]

    newton_root(stat, iterate, coupled)

    lower = pl.ds(HALF, HALF)
    upper = pl.ds(0, HALF)
    left_sent = remote(
        iterate.at[lower, :], root_other.at[upper, :], root_sem.at[0], root_sem.at[1], other_core
    )
    right_sent = remote(iterate, root_other, root_sem.at[0], root_sem.at[1], other_core)

    @pl.when(left_side)
    def _():
        left_sent.start()

    @pl.when(right_side)
    def _():
        right_sent.start()

    for c in range(2):
        origin = 2 * c + core

        @pl.when(origin == member)
        def _():
            piece_keep.wait()

        @pl.when(origin != member)
        def _():
            remote(pieces.at[c], pieces.at[c], piece_send.at[1], piece_recv.at[c], other_core).wait_recv()

    accum_load.wait()
    adagrad_total = jnp.zeros((1, 1), jnp.float32)
    for c in range(2):
        columns = slice(c * BLOCK, (c + 1) * BLOCK)
        squares = pieces[c] * pieces[c]
        grown = accum_here[:, columns] + squares
        new_accum[:, columns] = grown
        adagrad_total = adagrad_total + jnp.sum(squares / grown, keepdims=True)

    @pl.when(left_side)
    def _():
        rows = product(split(iterate[upper, :]), split(block[...]))
        left_sent.wait_send()
        right_sent.wait_recv()
        precond[...] = product(split(rows), split(root_other[...]))

    @pl.when(right_side)
    def _():
        columns = product(split(block[...]), split(iterate[...]))
        right_sent.wait_send()
        left_sent.wait_recv()
        precond[...] = product(split(root_other[upper, :]), split(columns))

    precond_total = jnp.sum(precond[...] * precond[...], keepdims=True)
    sums[...] = jnp.where(
        lax.broadcasted_iota(jnp.int32, sums.shape, 0) == 0, adagrad_total, precond_total
    )

    swap = remote(precond, other_block, swap_sem.at[0], swap_sem.at[1], swap_peer)

    @pl.when(swapped)
    def _():
        swap.start()

    def reduce_over(peers, source, slots, sends, recvs):
        copies = [
            remote(source, slots.at[j], sends.at[j], recvs.at[j], peer) for j, peer in enumerate(peers)
        ]
        for copy in copies:
            copy.start()
        total = source[...]
        for j, copy in enumerate(copies):
            copy.wait_recv()
            total = total + slots[j]
        return total, copies

    total, sent_mp = reduce_over(mp_peers, sums, mp_sums, mp_send, mp_recv)
    mp_total[...] = total
    total, sent_y = reduce_over(y_peers, mp_total, y_sums, ys_send, ys_recv)
    y_total[...] = total
    total, sent_z = reduce_over(z_peers, y_total, z_sums, zs_send, zs_recv)
    scale = jnp.sqrt(total[0:1, 0:1] / (total[1:2, 0:1] + 1e-12))

    @pl.when(swapped)
    def _():
        swap.wait()
        shard[...] = (other_block[...] * scale).astype(jnp.bfloat16)

    @pl.when(straight)
    def _():
        shard[...] = (precond[...] * scale).astype(jnp.bfloat16)

    first_row, row_count = (0, ROWS_A), (ROWS_A, ROWS_B)

    def region(part):
        kind, (a, b), half = part
        row, depth = wrap(y + a, NY), wrap(z + b, NZ)
        count = row_count[kind]
        begin = row * 1024 + depth // 4 * BLOCK + depth % 2 * HALF + first_row[kind]
        if half is not None:
            count //= 2
            begin = begin + half * count
        column = pl.multiple_of((depth // 2) % 2 * BLOCK, BLOCK)
        return out.at[pl.ds(pl.multiple_of(begin, 16), count), pl.ds(column, BLOCK)]

    start, events = spread_schedule()
    keys = [part for part, _ in events]
    sent = []

    def send(axis, sign, moved):
        kind, offsets, half = moved
        mine = list(offsets)
        mine[axis] += sign
        if offsets[axis] == (NY, NZ)[axis] // 2:
            mine[axis] = sign * offsets[axis] * -1 + sign
        mine = tuple(mine)
        here = region((kind, mine, half))
        if mine == (0, 0):
            count = row_count[kind] // (1 if half is None else 2)
            source = shard.at[pl.ds(first_row[kind] + (half or 0) * count, count), :]
        else:
            source = here
        target = (
            device(x, wrap(y + sign, NY), z, core) if axis == 0 else device(x, y, wrap(z + sign, NZ), core)
        )
        index = keys.index(moved)
        copy = remote(source, here, send_sem.at[index], recv_sem.at[index], target)
        copy.start()
        sent.append(copy)

    for one in start:
        send(*one)
    whole = pltpu.make_async_copy(
        shard,
        out.at[
            pl.ds(pl.multiple_of(y * 1024 + z // 4 * BLOCK + z % 2 * HALF, HALF), HALF),
            pl.ds(pl.multiple_of((z // 2) % 2 * BLOCK, BLOCK), BLOCK),
        ],
        local_sem.at[0],
    )
    whole.start()
    for index, (part, onward) in enumerate(events):
        here = region(part)
        remote(here, here, send_sem.at[index], recv_sem.at[index], swap_peer).wait_recv()
        for one in onward:
            send(*one)
    for copy in gather_sends + sent + sent_mp + sent_y + sent_z:
        copy.wait_send()
    gather_finish()
    whole.wait()

    @pl.when(swapped)
    def _():
        stat_back.wait()

    @pl.when(straight)
    def _():
        for copy in piece_copies:
            copy.wait_send()


def take_step(features, upstream, stats, accum):
    dma = pltpu.SemaphoreType.DMA
    tile = (8, 128)
    count = len(spread_schedule()[1])
    square = pltpu.VMEM((BLOCK, BLOCK), jnp.float32)
    vmem = pl.BlockSpec(memory_space=pltpu.VMEM)
    return pl.pallas_call(
        step_kernel,
        out_shape=(
            pltpu.VMEM((NY * NZ * 128, 1024), jnp.bfloat16),
            pltpu.VMEM((BLOCK, BLOCK), jnp.float32),
            pltpu.VMEM(accum.shape, jnp.float32),
        ),
        in_specs=[pl.BlockSpec(memory_space=pltpu.HBM)] * 4,
        out_specs=(vmem, vmem, vmem),
        scratch_shapes=[
            pltpu.VMEM((NZ, NY, NX, 16, BLOCK), jnp.bfloat16),
            pltpu.VMEM((NZ, NY, 64, BLOCK), jnp.bfloat16),
            pltpu.VMEM((NY, 16, 1024), jnp.bfloat16),
            pltpu.VMEM(accum.shape, jnp.float32),
            square, square, square, square, square, square, square, square,
            pltpu.VMEM((2, 128, BLOCK), jnp.float32),
            pltpu.VMEM((HALF, BLOCK), jnp.float32),
            pltpu.VMEM(tile, jnp.float32),
            pltpu.VMEM((HALF, BLOCK), jnp.float32),
            pltpu.VMEM((HALF, BLOCK), jnp.bfloat16),
            pltpu.VMEM((NX * NC, *tile), jnp.float32),
            pltpu.VMEM((NY, *tile), jnp.float32),
            pltpu.VMEM((NZ, *tile), jnp.float32),
            pltpu.VMEM(tile, jnp.float32),
            pltpu.VMEM(tile, jnp.float32),
            dma((NY,)), dma((NY,)), dma((NZ + 2,)), dma((NZ,)), dma((NZ, 4)), dma((NZ, 4)),
            dma((4, NC)), dma((NZ,)), dma((NZ, 4)), dma((NZ, 4)), dma((3,)),
            dma((2,)), dma((4,)), dma((4,)), dma((2,)), dma((4,)), dma((2,)), dma((2,)), dma((2,)),
            dma((NX * NC,)), dma((NX * NC,)), dma((NY,)), dma((NY,)), dma((NZ,)), dma((NZ,)),
            dma((2,)), dma((count,)), dma((count,)), dma((1,)),
        ],
        compiler_params=pltpu.CompilerParams(
            collective_id=0, has_side_effects=True, vmem_limit_bytes=50 * 2**20
        ),
    )(features, upstream, stats, accum)


def shards(features, upstream, stats, accum):
    update, new_stat, new_accum = take_step(features, upstream, stats[0, 0], accum)
    return (new_stat[None, None], new_accum, update)


def solution(mesh):
    placed = (P("dp", None), P("dp", "mp"), P("dp", "mp", None, None), P("dp", "mp"))
    return jax.shard_map(
        shards,
        mesh=mesh,
        in_specs=placed,
        out_specs=(P("dp", "mp", None, None), P("dp", "mp"), P(None, "mp")),
        check_vma=False,
    )
```

```python
import functools

import jax
import jax.numpy as jnp
from jax import lax
from jax.experimental import pallas as pl
from jax.experimental.pallas import tpu as pltpu
from jax.sharding import PartitionSpec as P

ITERS = 6
NX, NY, NZ, NC = 4, 4, 8, 2
MESH = pl.DeviceIdType.MESH
BLOCK = 512
HALF = BLOCK // 2
ROWS_A = 96
ROWS_B = HALF - ROWS_A


def place():
    dp, mp = lax.axis_index("dp"), lax.axis_index("mp")
    return mp // NC, dp // NZ, dp % NZ, mp % NC


def device(x, y, z, core):
    return (y * NZ + z, x * NC + core)


def wrap(value, size):
    return lax.rem(value + size, size)


def greet(partners):
    barrier = pltpu.get_barrier_semaphore()
    for partner in partners:
        pl.semaphore_signal(barrier, inc=1, device_id=partner, device_id_type=MESH)
    pl.semaphore_wait(barrier, len(partners))


def remote(src, dst, send_sem, recv_sem, target):
    return pltpu.make_async_remote_copy(
        src_ref=src,
        dst_ref=dst,
        send_sem=send_sem,
        recv_sem=recv_sem,
        device_id=target,
        device_id_type=MESH,
    )


def gather_block(
    features, upstream, partial, f_all, u_all, f_y,
    fy_send, fy_recv, fz_send, fz_recv, fx_send, fx_recv,
    uz_send, uz_recv, uy_send, uy_recv, keep_sem, send_stats,
):
    x, y, z, core = place()
    up, down, far_y = wrap(y + 1, NY), wrap(y - 1, NY), wrap(y + 2, NY)
    right, left, far_x = wrap(x + 1, NX), wrap(x - 1, NX), wrap(x + 2, NX)
    here = device(x, y, z, core)
    sends = []

    def go(copy):
        copy.start()
        sends.append(copy)

    def origin(d):
        return wrap(z - d, NZ)

    my_tokens = pl.ds(pl.multiple_of(64 * core + 16 * x, 16), 16)

    def f_cols(row):
        return features.at[my_tokens, pl.ds(pl.multiple_of(row * 1024, 1024), 1024)]

    def fy_start():
        for a in (2, 1, 3):
            row = wrap(y + a, NY)
            go(remote(f_cols(row), f_y.at[y], fy_send.at[a], fy_recv.at[a], device(x, row, z, core)))

    f_own = pltpu.make_async_copy(f_cols(y), f_y.at[y], keep_sem.at[0])

    def fy_wait():
        f_own.wait()
        for a in (1, 3, 2):
            into = f_y.at[wrap(y - a, NY)]
            remote(into, into, fy_send.at[a], fy_recv.at[a], here).wait_recv()

    def f_half(row):
        return f_y.at[:, :, pl.ds(pl.multiple_of(row // 4 * BLOCK, BLOCK), BLOCK)]

    f_keep = pltpu.make_async_copy(f_half(z), f_all.at[z, :, x], keep_sem.at[1])

    spot = z % 4
    maybe = []

    def go_if(condition, copy):
        pl.when(condition)(copy.start)
        maybe.append((condition, copy))

    def fz_copy(source, slot, d, row):
        into = f_all.at[wrap(row - d, NZ), :, x]
        return remote(source, into, fz_send.at[slot], fz_recv.at[d], device(x, y, row, core))

    def fz_start():
        above, below, two_up, two_down = (wrap(z + step, NZ) for step in (1, -1, 2, -2))
        go(fz_copy(f_half(above), 0, 1, above))
        go(fz_copy(f_half(below), 8, 7, below))
        go_if(spot == 1, fz_copy(f_half(two_down), 9, 6, two_down))
        go_if(spot == 2, fz_copy(f_half(two_up), 9, 2, two_up))

    def fz_pass(d):
        ref = f_all.at[origin(d), :, x]
        above, below = wrap(z + 1, NZ), wrap(z - 1, NZ)
        rising = {1: spot < 3, 2: spot < 3, 3: (spot == 1) | (spot == 2), 4: spot == 2}
        falling = {7: spot > 0, 6: spot > 0, 5: (spot == 1) | (spot == 2), 4: spot == 1}
        if d in rising:
            go_if(rising[d], fz_copy(ref, d, d + 1, above))
        if d in falling:
            go_if(falling[d], fz_copy(ref, d, d - 1, below))

    parity = wrap(core - z % NC, NC)
    on_chip = parity == 0

    def u_tile(token_half, row):
        column = pl.multiple_of((row // 2) % 2 * BLOCK, BLOCK)
        return upstream.at[pl.ds(64 * token_half, 64), pl.ds(column, BLOCK)]

    u_keep = pltpu.make_async_copy(u_tile(core, z), u_all.at[z, y], keep_sem.at[2])

    def u_remote(j, c):
        d = 2 * j + parity
        row = wrap(z + d, NZ)
        return remote(
            u_tile(c, row), u_all.at[z, y], uz_send.at[j, c], uz_recv.at[d], device(x, y, row, c)
        )

    def uz_start(*steps):
        for j in steps:
            for c in range(NC):
                copy = u_remote(j, c)
                if j == 0:
                    pl.when(jnp.logical_not(on_chip & (core == c)))(copy.start)
                else:
                    go(copy)

    def uz_finish():
        for c in range(NC):
            pl.when(jnp.logical_not(on_chip & (core == c)))(u_remote(0, c).wait_send)

    def u_part(d, row, part):
        ref = u_all.at[origin(d), row]
        return ref if part is None else ref.at[pl.ds(32 * part, 32), :]

    def u_copy(d, slot, row, part, target):
        ref = u_part(d, row, part)
        return remote(ref, ref, uy_send.at[d, slot], uy_recv.at[d, slot], device(x, target, z, core))

    def f_part(d, column, part):
        if part is None:
            return f_all.at[origin(d), :, column]
        return f_all.at[origin(d), pl.ds(2 * part, 2), column]

    def f_copy(d, slot, column, part, target):
        ref = f_part(d, column, part)
        return remote(ref, ref, fx_send.at[d, slot], fx_recv.at[d, slot], device(target, y, z, core))

    def u1(d):
        ref = u_all.at[origin(d), y]
        arrived = remote(ref, ref, uz_send.at[0, 0], uz_recv.at[d], here)
        if d == 0:
            pl.when(on_chip)(u_keep.wait)
            pl.when(jnp.logical_not(on_chip))(arrived.wait_recv)
        else:
            arrived.wait_recv()
        go(u_copy(d, 0, y, None, up))
        go(u_copy(d, 1, y, None, down))

    def u2(d):
        u_copy(d, 0, down, None, up).wait_recv()
        go(u_copy(d, 2, down, 0, up))
        u_copy(d, 1, up, None, down).wait_recv()
        go(u_copy(d, 3, up, 1, down))

    def f1(d):
        ref = f_all.at[origin(d), :, x]
        if d == 0:
            f_keep.wait()
        else:
            remote(ref, ref, fz_send.at[d], fz_recv.at[d], here).wait_recv()
            fz_pass(d)
        go(f_copy(d, 0, x, None, right))
        go(f_copy(d, 1, x, None, left))

    def f2(d):
        f_copy(d, 0, left, None, right).wait_recv()
        go(f_copy(d, 2, left, 0, right))
        f_copy(d, 1, right, None, left).wait_recv()
        go(f_copy(d, 3, right, 1, left))

    def add(d):
        for part in range(2):
            u_copy(d, 2 + part, far_y, part, up).wait_recv()
            f_copy(d, 2 + part, far_x, part, right).wait_recv()
        term = lax.dot_general(
            f_all[origin(d)].reshape(256, BLOCK),
            u_all[origin(d)].reshape(256, BLOCK),
            (((0,), (0,)), ((), ())),
            preferred_element_type=jnp.float32,
        )
        partial[...] = term if d == 0 else partial[...] + term

    fy_start()
    f_own.start()
    uz_start(0, 3, 1)
    pl.when(on_chip)(u_keep.start)
    fy_wait()
    fz_start()
    f_keep.start()
    send_stats()
    u1(0)
    f1(0)
    u1(1)
    u1(7)
    f1(1)
    f1(7)
    u1(6)
    uz_start(2)
    for d in (0, 1, 7):
        u2(d)
        f2(d)
    f1(2)
    f1(6)
    u1(2)
    u1(3)
    u2(6)
    f2(2)
    f2(6)
    f1(3)
    f1(5)
    u2(2)
    u2(3)
    u1(5)
    u1(4)
    add(0)
    f1(4)
    f2(3)
    f2(5)
    add(1)
    u2(5)
    u2(4)
    f2(4)
    for d in (7, 6, 2, 3, 5, 4):
        add(d)

    def finish():
        uz_finish()
        for condition, copy in maybe:
            pl.when(condition)(copy.wait_send)

    return sends, finish


def spread_plan():
    rows = (ROWS_A, ROWS_B)
    first, second = (0, 1), (1, 0)
    sizes = (NY, NZ)

    def onward(part):
        kind, offsets, half = part
        out = []
        for level, axis in enumerate((first, second)[kind]):
            far = sizes[axis] // 2
            offset = offsets[axis]
            later = (first, second)[kind][level + 1 :]
            if any(offsets[other] != 0 for other in later):
                continue
            for sign in (1, -1):
                if offset * sign > 0 or abs(offset) == far:
                    continue
                moved = list(offsets)
                moved[axis] = offset - sign
                if abs(moved[axis]) == far:
                    moved[axis] = far
                    out.append((axis, sign, (kind, tuple(moved), 0 if sign == 1 else 1)))
                else:
                    out.append((axis, sign, (kind, tuple(moved), None)))
        return out

    return rows, onward


def spread_schedule():
    rows, onward = spread_plan()
    link_free = {}
    events = []
    pending = []
    halves = {}

    def launch(time, part):
        sends = []
        for axis, sign, moved in onward(part):
            count = rows[moved[0]] // (1 if moved[2] is None else 2)
            begin = max(time, link_free.get((axis, sign), 0.0))
            done = begin + count * BLOCK * 2 * 2 / 100e3
            link_free[(axis, sign)] = done
            pending.append((done + 1.0, len(pending), moved))
            sends.append((axis, sign, moved))
        return sends

    start = [launch(0.0, (kind, (0, 0), None)) for kind in (1, 0)]
    while pending:
        pending.sort()
        time, _, part = pending.pop(0)
        kind, offsets, half = part
        if half is not None:
            halves[(kind, offsets)] = halves.get((kind, offsets), 0) + 1
            if halves[(kind, offsets)] == 2:
                events.append((part, launch(time, (kind, offsets, None))))
            else:
                events.append((part, []))
        else:
            events.append((part, launch(time, part)))
    return [send for group in start for send in group], events


def split(value):
    high = value.astype(jnp.bfloat16)
    return high, (value - high.astype(jnp.float32)).astype(jnp.bfloat16)


def product(first, second):
    dot = functools.partial(jnp.dot, preferred_element_type=jnp.float32)
    return dot(first[0], second[0]) + (dot(first[0], second[1]) + dot(first[1], second[0]))


def symmetric_product(first, second):
    left = product(first, [part[:, :HALF] for part in second])
    last = product([part[HALF:] for part in first], [part[:, HALF:] for part in second])
    return jnp.concatenate([left, jnp.concatenate([left[HALF:].T, last], 0)], 1)


def newton_root(stat, iterate, coupled):
    def advance(now, now_parts):
        change = split((symmetric_product(now_parts, now_parts) - 10.0 * now) * (1 / 16))
        once = (25 / 16) * now + symmetric_product(change, now_parts)
        return (25 / 16) * once + symmetric_product(change, split(once))

    start = stat[...]
    factor = 2.5 / jnp.sqrt(jnp.sum(start * start, keepdims=True))
    start = start * factor
    shape = (BLOCK, BLOCK)
    diagonal = lax.broadcasted_iota(jnp.int32, shape, 0) == lax.broadcasted_iota(jnp.int32, shape, 1)
    iterate[...] = jnp.sqrt(jnp.sqrt(factor)) * (jnp.where(diagonal, 1.25, 0.0) - 0.25 * start)
    coupled[...] = advance(start, split(start))

    def body(_, carry):
        now, root = coupled[...], iterate[...]
        now_parts = split(now)
        iterate[...] = 1.25 * root - 0.25 * symmetric_product(split(root), now_parts)
        coupled[...] = advance(now, now_parts)
        return carry

    lax.fori_loop(0, ITERS - 2, body, 0)
    root = iterate[...]
    iterate[...] = 1.25 * root - 0.25 * symmetric_product(split(root), split(coupled[...]))


def step_kernel(
    features, upstream, stats, accum, out, new_stat, new_accum,
    f_all, u_all, f_y, accum_here, stat_other, partial, partial_other, block, stat, iterate, coupled, root_other, pieces, precond, sums,
    other_block, shard, mp_sums, y_sums, z_sums, mp_total, y_total,
    fy_send, fy_recv, fz_send, fz_recv, fx_send, fx_recv, uz_send, uz_recv, uy_send, uy_recv, keep_sem,
    load_sem, stats_send, stats_recv, core_sem, piece_send, piece_recv, stat_sem, root_sem,
    mp_send, mp_recv, ys_send, ys_recv, zs_send, zs_recv, swap_sem, send_sem, recv_sem, local_sem,
):
    x, y, z, core = place()
    mp = x * NC + core
    mp_peers = [(y * NZ + z, wrap(mp + j, NX * NC)) for j in range(1, NX * NC)]
    y_peers = [device(x, wrap(y + j, NY), z, core) for j in range(1, NY)]
    z_peers = [device(x, y, wrap(z + j, NZ), core) for j in range(1, NZ)]
    swapped = z % NC != core
    straight = jnp.logical_not(swapped)
    left_side = core == 0
    right_side = core == 1
    other_core = device(x, y, z, 1 - core)
    swap_peer = device(x, y, z + 1 - 2 * (z % NC), 1 - core)
    across = [device(x, y, wrap(z + j, NZ), 1 - core) for j in range(1, NZ)]
    greet(mp_peers + y_peers + z_peers + across)
    accum_load = pltpu.make_async_copy(accum, accum_here, load_sem.at[0])
    stat_load = pltpu.make_async_copy(stats, stat, load_sem.at[1])
    accum_load.start()
    pl.when(straight)(stat_load.start)

    stat_copies = []
    for i in range(4):
        at = pl.ds(128 * i, 128), pl.ds(128 * i, BLOCK - 128 * i)
        stat_copies.append(
            remote(stats.at[at], stat_other.at[at], stats_send.at[i], stats_recv.at[i], swap_peer)
        )

    def send_stats():
        for copy in stat_copies:
            pl.when(swapped)(copy.start)

    gather_sends, gather_finish = gather_block(
        features, upstream, partial, f_all, u_all, f_y,
        fy_send, fy_recv, fz_send, fz_recv, fx_send, fx_recv,
        uz_send, uz_recv, uy_send, uy_recv, keep_sem, send_stats,
    )

    exchange = remote(partial, partial_other, core_sem.at[0], core_sem.at[1], other_core)
    exchange.start()

    @pl.when(swapped)
    def _():
        for copy in stat_copies:
            copy.wait()
        for i in range(1, 4):
            for j in range(i):
                stat_other[128 * i : 128 * i + 128, 128 * j : 128 * j + 128] = stat_other[
                    128 * j : 128 * j + 128, 128 * i : 128 * i + 128
                ].T
        stat[...] = stat_other[...]

    @pl.when(straight)
    def _():
        stat_load.wait()

    exchange.wait()
    both = partial[...] + partial_other[...]
    block[...] = both

    member, quad, column = z % 4, z // 4 * 4, (z // 2) % 2

    def piece_rows(row):
        return block.at[pl.ds(pl.multiple_of(row * 128, 128), 128), :]

    piece_copies = []
    for j in range(1, 4):
        row = wrap(member + j, 4)
        piece_copies.append(
            remote(
                piece_rows(row), pieces.at[column], piece_send.at[j], piece_recv.at[column],
                device(x, y, quad + row, core),
            )
        )
    piece_keep = pltpu.make_async_copy(piece_rows(member), pieces.at[column], piece_send.at[0])

    @pl.when(straight)
    def _():
        for copy in piece_copies:
            copy.start()
        piece_keep.start()

    turned = both.T
    first = jnp.where(left_side, both, turned)
    second = jnp.where(left_side, turned, both)
    stat[...] = stat[...] + symmetric_product(split(first), split(second))
    stat_back = remote(stat, new_stat, stat_sem.at[0], stat_sem.at[1], swap_peer)

    @pl.when(swapped)
    def _():
        stat_back.start()

    @pl.when(straight)
    def _():
        new_stat[...] = stat[...]

    newton_root(stat, iterate, coupled)

    lower = pl.ds(HALF, HALF)
    upper = pl.ds(0, HALF)
    left_sent = remote(
        iterate.at[lower, :], root_other.at[upper, :], root_sem.at[0], root_sem.at[1], other_core
    )
    right_sent = remote(iterate, root_other, root_sem.at[0], root_sem.at[1], other_core)

    @pl.when(left_side)
    def _():
        left_sent.start()

    @pl.when(right_side)
    def _():
        right_sent.start()

    for c in range(2):
        origin = 2 * c + core

        @pl.when(origin == member)
        def _():
            piece_keep.wait()

        @pl.when(origin != member)
        def _():
            remote(pieces.at[c], pieces.at[c], piece_send.at[1], piece_recv.at[c], other_core).wait_recv()

    accum_load.wait()
    adagrad_total = jnp.zeros((1, 1), jnp.float32)
    for c in range(2):
        columns = slice(c * BLOCK, (c + 1) * BLOCK)
        squares = pieces[c] * pieces[c]
        grown = accum_here[:, columns] + squares
        new_accum[:, columns] = grown
        adagrad_total = adagrad_total + jnp.sum(squares / grown, keepdims=True)

    @pl.when(left_side)
    def _():
        rows = product(split(iterate[upper, :]), split(block[...]))
        left_sent.wait_send()
        right_sent.wait_recv()
        precond[...] = product(split(rows), split(root_other[...]))

    @pl.when(right_side)
    def _():
        columns = product(split(block[...]), split(iterate[...]))
        right_sent.wait_send()
        left_sent.wait_recv()
        precond[...] = product(split(root_other[upper, :]), split(columns))

    precond_total = jnp.sum(precond[...] * precond[...], keepdims=True)
    sums[...] = jnp.where(
        lax.broadcasted_iota(jnp.int32, sums.shape, 0) == 0, adagrad_total, precond_total
    )

    swap = remote(precond, other_block, swap_sem.at[0], swap_sem.at[1], swap_peer)

    @pl.when(swapped)
    def _():
        swap.start()

    def reduce_over(peers, source, slots, sends, recvs):
        copies = [
            remote(source, slots.at[j], sends.at[j], recvs.at[j], peer) for j, peer in enumerate(peers)
        ]
        for copy in copies:
            copy.start()
        total = source[...]
        for j, copy in enumerate(copies):
            copy.wait_recv()
            total = total + slots[j]
        return total, copies

    total, sent_mp = reduce_over(mp_peers, sums, mp_sums, mp_send, mp_recv)
    mp_total[...] = total
    total, sent_y = reduce_over(y_peers, mp_total, y_sums, ys_send, ys_recv)
    y_total[...] = total
    total, sent_z = reduce_over(z_peers, y_total, z_sums, zs_send, zs_recv)
    scale = jnp.sqrt(total[0:1, 0:1] / (total[1:2, 0:1] + 1e-12))

    @pl.when(swapped)
    def _():
        swap.wait()
        shard[...] = (other_block[...] * scale).astype(jnp.bfloat16)

    @pl.when(straight)
    def _():
        shard[...] = (precond[...] * scale).astype(jnp.bfloat16)

    first_row, row_count = (0, ROWS_A), (ROWS_A, ROWS_B)

    def region(part):
        kind, (a, b), half = part
        row, depth = wrap(y + a, NY), wrap(z + b, NZ)
        count = row_count[kind]
        begin = row * 1024 + depth // 4 * BLOCK + depth % 2 * HALF + first_row[kind]
        if half is not None:
            count //= 2
            begin = begin + half * count
        column = pl.multiple_of((depth // 2) % 2 * BLOCK, BLOCK)
        return out.at[pl.ds(pl.multiple_of(begin, 16), count), pl.ds(column, BLOCK)]

    start, events = spread_schedule()
    keys = [part for part, _ in events]
    sent = []

    def send(axis, sign, moved):
        kind, offsets, half = moved
        mine = list(offsets)
        mine[axis] += sign
        if offsets[axis] == (NY, NZ)[axis] // 2:
            mine[axis] = sign * offsets[axis] * -1 + sign
        mine = tuple(mine)
        here = region((kind, mine, half))
        if mine == (0, 0):
            count = row_count[kind] // (1 if half is None else 2)
            source = shard.at[pl.ds(first_row[kind] + (half or 0) * count, count), :]
        else:
            source = here
        target = (
            device(x, wrap(y + sign, NY), z, core) if axis == 0 else device(x, y, wrap(z + sign, NZ), core)
        )
        index = keys.index(moved)
        copy = remote(source, here, send_sem.at[index], recv_sem.at[index], target)
        copy.start()
        sent.append(copy)

    for one in start:
        send(*one)
    whole = pltpu.make_async_copy(
        shard,
        out.at[
            pl.ds(pl.multiple_of(y * 1024 + z // 4 * BLOCK + z % 2 * HALF, HALF), HALF),
            pl.ds(pl.multiple_of((z // 2) % 2 * BLOCK, BLOCK), BLOCK),
        ],
        local_sem.at[0],
    )
    whole.start()
    for index, (part, onward) in enumerate(events):
        here = region(part)
        remote(here, here, send_sem.at[index], recv_sem.at[index], swap_peer).wait_recv()
        for one in onward:
            send(*one)
    for copy in gather_sends + sent + sent_mp + sent_y + sent_z:
        copy.wait_send()
    gather_finish()
    whole.wait()

    @pl.when(swapped)
    def _():
        stat_back.wait()

    @pl.when(straight)
    def _():
        for copy in piece_copies:
            copy.wait_send()


def take_step(features, upstream, stats, accum):
    dma = pltpu.SemaphoreType.DMA
    tile = (8, 128)
    count = len(spread_schedule()[1])
    square = pltpu.VMEM((BLOCK, BLOCK), jnp.float32)
    vmem = pl.BlockSpec(memory_space=pltpu.VMEM)
    return pl.pallas_call(
        step_kernel,
        out_shape=(
            pltpu.VMEM((NY * NZ * 128, 1024), jnp.bfloat16),
            pltpu.VMEM((BLOCK, BLOCK), jnp.float32),
            pltpu.VMEM(accum.shape, jnp.float32),
        ),
        in_specs=[pl.BlockSpec(memory_space=pltpu.HBM)] * 4,
        out_specs=(vmem, vmem, vmem),
        scratch_shapes=[
            pltpu.VMEM((NZ, NY, NX, 16, BLOCK), jnp.bfloat16),
            pltpu.VMEM((NZ, NY, 64, BLOCK), jnp.bfloat16),
            pltpu.VMEM((NY, 16, 1024), jnp.bfloat16),
            pltpu.VMEM(accum.shape, jnp.float32),
            square, square, square, square, square, square, square, square,
            pltpu.VMEM((2, 128, BLOCK), jnp.float32),
            pltpu.VMEM((HALF, BLOCK), jnp.float32),
            pltpu.VMEM(tile, jnp.float32),
            pltpu.VMEM((HALF, BLOCK), jnp.float32),
            pltpu.VMEM((HALF, BLOCK), jnp.bfloat16),
            pltpu.VMEM((NX * NC, *tile), jnp.float32),
            pltpu.VMEM((NY, *tile), jnp.float32),
            pltpu.VMEM((NZ, *tile), jnp.float32),
            pltpu.VMEM(tile, jnp.float32),
            pltpu.VMEM(tile, jnp.float32),
            dma((NY,)), dma((NY,)), dma((NZ + 2,)), dma((NZ,)), dma((NZ, 4)), dma((NZ, 4)),
            dma((4, NC)), dma((NZ,)), dma((NZ, 4)), dma((NZ, 4)), dma((3,)),
            dma((2,)), dma((4,)), dma((4,)), dma((2,)), dma((4,)), dma((2,)), dma((2,)), dma((2,)),
            dma((NX * NC,)), dma((NX * NC,)), dma((NY,)), dma((NY,)), dma((NZ,)), dma((NZ,)),
            dma((2,)), dma((count,)), dma((count,)), dma((1,)),
        ],
        compiler_params=pltpu.CompilerParams(
            collective_id=0, has_side_effects=True, vmem_limit_bytes=50 * 2**20
        ),
    )(features, upstream, stats, accum)


def deliver_kernel(update, stat, accum, update_out, stat_out, accum_out, sems):
    copies = []

    def go(source, into):
        copy = pltpu.make_async_copy(source, into, sems.at[len(copies)])
        copy.start()
        copies.append(copy)

    for part in range(8):
        rows = pl.ds(part * 512, 512)
        go(update.at[rows, :], update_out.at[rows, :])
    go(stat, stat_out)
    go(accum, accum_out)
    for copy in copies:
        copy.wait()


def deliver(update, stat, accum):
    return pl.pallas_call(
        deliver_kernel,
        out_shape=tuple(jax.ShapeDtypeStruct(one.shape, one.dtype) for one in (update, stat, accum)),
        in_specs=[pl.BlockSpec(memory_space=pl.ANY)] * 3,
        out_specs=(pl.BlockSpec(memory_space=pltpu.HBM),) * 3,
        scratch_shapes=[pltpu.SemaphoreType.DMA((10,))],
    )(update, stat, accum)


def shards(features, upstream, stats, accum):
    update, new_stat, new_accum = deliver(*take_step(features, upstream, stats[0, 0], accum))
    return (new_stat[None, None], new_accum, update)


def solution(mesh):
    placed = (P("dp", None), P("dp", "mp"), P("dp", "mp", None, None), P("dp", "mp"))
    return jax.shard_map(
        shards,
        mesh=mesh,
        in_specs=placed,
        out_specs=(P("dp", "mp", None, None), P("dp", "mp"), P(None, "mp")),
        check_vma=False,
    )
```

```python
import functools

import jax
import jax.numpy as jnp
from jax import lax
from jax.experimental import pallas as pl
from jax.experimental.pallas import tpu as pltpu
from jax.sharding import PartitionSpec as P

ITERS = 6
NX, NY, NZ, NC = 4, 4, 8, 2
MESH = pl.DeviceIdType.MESH
BLOCK = 512
HALF = BLOCK // 2
ROWS_A = 96
ROWS_B = HALF - ROWS_A


def place():
    dp, mp = lax.axis_index("dp"), lax.axis_index("mp")
    return mp // NC, dp // NZ, dp % NZ, mp % NC


def device(x, y, z, core):
    return (y * NZ + z, x * NC + core)


def wrap(value, size):
    return lax.rem(value + size, size)


def greet(partners):
    barrier = pltpu.get_barrier_semaphore()
    for partner in partners:
        pl.semaphore_signal(barrier, inc=1, device_id=partner, device_id_type=MESH)
    pl.semaphore_wait(barrier, len(partners))


def remote(src, dst, send_sem, recv_sem, target):
    return pltpu.make_async_remote_copy(
        src_ref=src,
        dst_ref=dst,
        send_sem=send_sem,
        recv_sem=recv_sem,
        device_id=target,
        device_id_type=MESH,
    )


def gather_block(
    features, upstream, partial, f_all, u_all, f_y,
    fy_send, fy_recv, fz_send, fz_recv, fx_send, fx_recv,
    uz_send, uz_recv, uy_send, uy_recv, keep_sem, send_stats,
):
    x, y, z, core = place()
    up, down, far_y = wrap(y + 1, NY), wrap(y - 1, NY), wrap(y + 2, NY)
    right, left, far_x = wrap(x + 1, NX), wrap(x - 1, NX), wrap(x + 2, NX)
    here = device(x, y, z, core)
    sends = []

    def go(copy):
        copy.start()
        sends.append(copy)

    def origin(d):
        return wrap(z - d, NZ)

    my_tokens = pl.ds(pl.multiple_of(64 * core + 16 * x, 16), 16)

    def f_cols(row):
        return features.at[my_tokens, pl.ds(pl.multiple_of(row * 1024, 1024), 1024)]

    def fy_start():
        for a in (2, 1, 3):
            row = wrap(y + a, NY)
            go(remote(f_cols(row), f_y.at[y], fy_send.at[a], fy_recv.at[a], device(x, row, z, core)))

    f_own = pltpu.make_async_copy(f_cols(y), f_y.at[y], keep_sem.at[0])

    def fy_wait():
        f_own.wait()
        for a in (1, 3, 2):
            into = f_y.at[wrap(y - a, NY)]
            remote(into, into, fy_send.at[a], fy_recv.at[a], here).wait_recv()

    def f_half(row):
        return f_y.at[:, :, pl.ds(pl.multiple_of(row // 4 * BLOCK, BLOCK), BLOCK)]

    f_keep = pltpu.make_async_copy(f_half(z), f_all.at[z, :, x], keep_sem.at[1])

    spot = z % 4
    maybe = []

    def go_if(condition, copy):
        pl.when(condition)(copy.start)
        maybe.append((condition, copy))

    def fz_copy(source, slot, d, row):
        into = f_all.at[wrap(row - d, NZ), :, x]
        return remote(source, into, fz_send.at[slot], fz_recv.at[d], device(x, y, row, core))

    def fz_start():
        above, below, two_up, two_down = (wrap(z + step, NZ) for step in (1, -1, 2, -2))
        go(fz_copy(f_half(above), 0, 1, above))
        go(fz_copy(f_half(below), 8, 7, below))
        go_if(spot == 1, fz_copy(f_half(two_down), 9, 6, two_down))
        go_if(spot == 2, fz_copy(f_half(two_up), 9, 2, two_up))

    def fz_pass(d):
        ref = f_all.at[origin(d), :, x]
        above, below = wrap(z + 1, NZ), wrap(z - 1, NZ)
        rising = {1: spot < 3, 2: spot < 3, 3: (spot == 1) | (spot == 2), 4: spot == 2}
        falling = {7: spot > 0, 6: spot > 0, 5: (spot == 1) | (spot == 2), 4: spot == 1}
        if d in rising:
            go_if(rising[d], fz_copy(ref, d, d + 1, above))
        if d in falling:
            go_if(falling[d], fz_copy(ref, d, d - 1, below))

    parity = wrap(core - z % NC, NC)
    on_chip = parity == 0

    def u_tile(token_half, row):
        column = pl.multiple_of((row // 2) % 2 * BLOCK, BLOCK)
        return upstream.at[pl.ds(64 * token_half, 64), pl.ds(column, BLOCK)]

    u_keep = pltpu.make_async_copy(u_tile(core, z), u_all.at[z, y], keep_sem.at[2])

    def u_remote(j, c):
        d = 2 * j + parity
        row = wrap(z + d, NZ)
        return remote(
            u_tile(c, row), u_all.at[z, y], uz_send.at[j, c], uz_recv.at[d], device(x, y, row, c)
        )

    def uz_start(*steps):
        for j in steps:
            for c in range(NC):
                copy = u_remote(j, c)
                if j == 0:
                    pl.when(jnp.logical_not(on_chip & (core == c)))(copy.start)
                else:
                    go(copy)

    def uz_finish():
        for c in range(NC):
            pl.when(jnp.logical_not(on_chip & (core == c)))(u_remote(0, c).wait_send)

    def u_part(d, row, part):
        ref = u_all.at[origin(d), row]
        return ref if part is None else ref.at[pl.ds(32 * part, 32), :]

    def u_copy(d, slot, row, part, target):
        ref = u_part(d, row, part)
        return remote(ref, ref, uy_send.at[d, slot], uy_recv.at[d, slot], device(x, target, z, core))

    def f_part(d, column, part):
        if part is None:
            return f_all.at[origin(d), :, column]
        return f_all.at[origin(d), pl.ds(2 * part, 2), column]

    def f_copy(d, slot, column, part, target):
        ref = f_part(d, column, part)
        return remote(ref, ref, fx_send.at[d, slot], fx_recv.at[d, slot], device(target, y, z, core))

    def u1(d):
        ref = u_all.at[origin(d), y]
        arrived = remote(ref, ref, uz_send.at[0, 0], uz_recv.at[d], here)
        if d == 0:
            pl.when(on_chip)(u_keep.wait)
            pl.when(jnp.logical_not(on_chip))(arrived.wait_recv)
        else:
            arrived.wait_recv()
        go(u_copy(d, 0, y, None, up))
        go(u_copy(d, 1, y, None, down))

    def u2(d):
        u_copy(d, 0, down, None, up).wait_recv()
        go(u_copy(d, 2, down, 0, up))
        u_copy(d, 1, up, None, down).wait_recv()
        go(u_copy(d, 3, up, 1, down))

    def f1(d):
        ref = f_all.at[origin(d), :, x]
        if d == 0:
            f_keep.wait()
        else:
            remote(ref, ref, fz_send.at[d], fz_recv.at[d], here).wait_recv()
            fz_pass(d)
        go(f_copy(d, 0, x, None, right))
        go(f_copy(d, 1, x, None, left))

    def f2(d):
        f_copy(d, 0, left, None, right).wait_recv()
        go(f_copy(d, 2, left, 0, right))
        f_copy(d, 1, right, None, left).wait_recv()
        go(f_copy(d, 3, right, 1, left))

    def add(d):
        for part in range(2):
            u_copy(d, 2 + part, far_y, part, up).wait_recv()
            f_copy(d, 2 + part, far_x, part, right).wait_recv()
        term = lax.dot_general(
            f_all[origin(d)].reshape(256, BLOCK),
            u_all[origin(d)].reshape(256, BLOCK),
            (((0,), (0,)), ((), ())),
            preferred_element_type=jnp.float32,
        )
        partial[...] = term if d == 0 else partial[...] + term

    fy_start()
    f_own.start()
    uz_start(0, 3)
    pl.when(on_chip)(u_keep.start)
    fy_wait()
    fz_start()
    f_keep.start()
    u1(0)
    f1(0)
    uz_start(1)
    u1(1)
    u1(7)
    f1(1)
    f1(7)
    u1(6)
    uz_start(2)
    for d in (0, 1, 7):
        u2(d)
        f2(d)
    f1(2)
    f1(6)
    u1(2)
    u1(3)
    u2(6)
    f2(2)
    f2(6)
    send_stats()
    f1(3)
    f1(5)
    u2(2)
    u2(3)
    u1(5)
    u1(4)
    add(0)
    f1(4)
    f2(3)
    f2(5)
    add(1)
    u2(5)
    u2(4)
    f2(4)
    for d in (7, 6, 2, 3, 5, 4):
        add(d)

    def finish():
        uz_finish()
        for condition, copy in maybe:
            pl.when(condition)(copy.wait_send)

    return sends, finish


def spread_plan():
    rows = (ROWS_A, ROWS_B)
    first, second = (0, 1), (1, 0)
    sizes = (NY, NZ)

    def onward(part):
        kind, offsets, half = part
        out = []
        for level, axis in enumerate((first, second)[kind]):
            far = sizes[axis] // 2
            offset = offsets[axis]
            later = (first, second)[kind][level + 1 :]
            if any(offsets[other] != 0 for other in later):
                continue
            for sign in (1, -1):
                if offset * sign > 0 or abs(offset) == far:
                    continue
                moved = list(offsets)
                moved[axis] = offset - sign
                if abs(moved[axis]) == far:
                    moved[axis] = far
                    out.append((axis, sign, (kind, tuple(moved), 0 if sign == 1 else 1)))
                else:
                    out.append((axis, sign, (kind, tuple(moved), None)))
        return out

    return rows, onward


def spread_schedule():
    rows, onward = spread_plan()
    link_free = {}
    events = []
    pending = []
    halves = {}

    def launch(time, part):
        sends = []
        for axis, sign, moved in onward(part):
            count = rows[moved[0]] // (1 if moved[2] is None else 2)
            begin = max(time, link_free.get((axis, sign), 0.0))
            done = begin + count * BLOCK * 2 * 2 / 100e3
            link_free[(axis, sign)] = done
            pending.append((done + 1.0, len(pending), moved))
            sends.append((axis, sign, moved))
        return sends

    start = [launch(0.0, (kind, (0, 0), None)) for kind in (1, 0)]
    while pending:
        pending.sort()
        time, _, part = pending.pop(0)
        kind, offsets, half = part
        if half is not None:
            halves[(kind, offsets)] = halves.get((kind, offsets), 0) + 1
            if halves[(kind, offsets)] == 2:
                events.append((part, launch(time, (kind, offsets, None))))
            else:
                events.append((part, []))
        else:
            events.append((part, launch(time, part)))
    return [send for group in start for send in group], events


def split(value):
    high = value.astype(jnp.bfloat16)
    return high, (value - high.astype(jnp.float32)).astype(jnp.bfloat16)


def product(first, second):
    dot = functools.partial(jnp.dot, preferred_element_type=jnp.float32)
    return dot(first[0], second[0]) + (dot(first[0], second[1]) + dot(first[1], second[0]))


def symmetric_product(first, second):
    left = product(first, [part[:, :HALF] for part in second])
    last = product([part[HALF:] for part in first], [part[:, HALF:] for part in second])
    return jnp.concatenate([left, jnp.concatenate([left[HALF:].T, last], 0)], 1)


def newton_root(stat, iterate, coupled):
    def advance(now, now_parts):
        change = split((symmetric_product(now_parts, now_parts) - 10.0 * now) * (1 / 16))
        once = (25 / 16) * now + symmetric_product(change, now_parts)
        return (25 / 16) * once + symmetric_product(change, split(once))

    start = stat[...]
    factor = 2.5 / jnp.sqrt(jnp.sum(start * start, keepdims=True))
    start = start * factor
    shape = (BLOCK, BLOCK)
    diagonal = lax.broadcasted_iota(jnp.int32, shape, 0) == lax.broadcasted_iota(jnp.int32, shape, 1)
    iterate[...] = jnp.sqrt(jnp.sqrt(factor)) * (jnp.where(diagonal, 1.25, 0.0) - 0.25 * start)
    coupled[...] = advance(start, split(start))

    def body(_, carry):
        now, root = coupled[...], iterate[...]
        now_parts = split(now)
        iterate[...] = 1.25 * root - 0.25 * symmetric_product(split(root), now_parts)
        coupled[...] = advance(now, now_parts)
        return carry

    lax.fori_loop(0, ITERS - 2, body, 0)
    root = iterate[...]
    iterate[...] = 1.25 * root - 0.25 * symmetric_product(split(root), split(coupled[...]))


def step_kernel(
    features, upstream, stats, accum, out, new_stat, new_accum,
    f_all, u_all, f_y, accum_here, stat_other, partial, partial_other, block, stat, iterate, coupled, root_other, pieces, precond, sums,
    other_block, shard, mp_sums, y_sums, z_sums, mp_total, y_total,
    fy_send, fy_recv, fz_send, fz_recv, fx_send, fx_recv, uz_send, uz_recv, uy_send, uy_recv, keep_sem,
    load_sem, stats_send, stats_recv, core_sem, piece_send, piece_recv, stat_sem, root_sem,
    mp_send, mp_recv, ys_send, ys_recv, zs_send, zs_recv, swap_sem, send_sem, recv_sem, local_sem,
):
    x, y, z, core = place()
    mp = x * NC + core
    mp_peers = [(y * NZ + z, wrap(mp + j, NX * NC)) for j in range(1, NX * NC)]
    y_peers = [device(x, wrap(y + j, NY), z, core) for j in range(1, NY)]
    z_peers = [device(x, y, wrap(z + j, NZ), core) for j in range(1, NZ)]
    swapped = z % NC != core
    straight = jnp.logical_not(swapped)
    left_side = core == 0
    right_side = core == 1
    other_core = device(x, y, z, 1 - core)
    swap_peer = device(x, y, z + 1 - 2 * (z % NC), 1 - core)
    across = [device(x, y, wrap(z + j, NZ), 1 - core) for j in range(1, NZ)]
    greet(mp_peers + y_peers + z_peers + across)
    accum_load = pltpu.make_async_copy(accum, accum_here, load_sem.at[0])
    stat_load = pltpu.make_async_copy(stats, stat, load_sem.at[1])
    accum_load.start()
    pl.when(straight)(stat_load.start)

    stat_copies = []
    for i in range(4):
        at = pl.ds(128 * i, 128), pl.ds(128 * i, BLOCK - 128 * i)
        stat_copies.append(
            remote(stats.at[at], stat_other.at[at], stats_send.at[i], stats_recv.at[i], swap_peer)
        )

    def send_stats():
        for copy in stat_copies:
            pl.when(swapped)(copy.start)

    gather_sends, gather_finish = gather_block(
        features, upstream, partial, f_all, u_all, f_y,
        fy_send, fy_recv, fz_send, fz_recv, fx_send, fx_recv,
        uz_send, uz_recv, uy_send, uy_recv, keep_sem, send_stats,
    )

    exchange = remote(partial, partial_other, core_sem.at[0], core_sem.at[1], other_core)
    exchange.start()

    @pl.when(swapped)
    def _():
        for copy in stat_copies:
            copy.wait()
        for i in range(1, 4):
            for j in range(i):
                stat_other[128 * i : 128 * i + 128, 128 * j : 128 * j + 128] = stat_other[
                    128 * j : 128 * j + 128, 128 * i : 128 * i + 128
                ].T
        stat[...] = stat_other[...]

    @pl.when(straight)
    def _():
        stat_load.wait()

    exchange.wait()
    both = partial[...] + partial_other[...]
    block[...] = both

    member, quad, column = z % 4, z // 4 * 4, (z // 2) % 2

    def piece_rows(row):
        return block.at[pl.ds(pl.multiple_of(row * 128, 128), 128), :]

    piece_copies = []
    for j in range(1, 4):
        row = wrap(member + j, 4)
        piece_copies.append(
            remote(
                piece_rows(row), pieces.at[column], piece_send.at[j], piece_recv.at[column],
                device(x, y, quad + row, core),
            )
        )
    piece_keep = pltpu.make_async_copy(piece_rows(member), pieces.at[column], piece_send.at[0])

    @pl.when(straight)
    def _():
        for copy in piece_copies:
            copy.start()
        piece_keep.start()

    turned = both.T
    first = jnp.where(left_side, both, turned)
    second = jnp.where(left_side, turned, both)
    stat[...] = stat[...] + symmetric_product(split(first), split(second))
    stat_back = remote(stat, new_stat, stat_sem.at[0], stat_sem.at[1], swap_peer)

    @pl.when(swapped)
    def _():
        stat_back.start()

    @pl.when(straight)
    def _():
        new_stat[...] = stat[...]

    newton_root(stat, iterate, coupled)

    lower = pl.ds(HALF, HALF)
    upper = pl.ds(0, HALF)
    left_sent = remote(
        iterate.at[lower, :], root_other.at[upper, :], root_sem.at[0], root_sem.at[1], other_core
    )
    right_sent = remote(iterate, root_other, root_sem.at[0], root_sem.at[1], other_core)

    @pl.when(left_side)
    def _():
        left_sent.start()

    @pl.when(right_side)
    def _():
        right_sent.start()

    for c in range(2):
        origin = 2 * c + core

        @pl.when(origin == member)
        def _():
            piece_keep.wait()

        @pl.when(origin != member)
        def _():
            remote(pieces.at[c], pieces.at[c], piece_send.at[1], piece_recv.at[c], other_core).wait_recv()

    accum_load.wait()
    adagrad_total = jnp.zeros((1, 1), jnp.float32)
    for c in range(2):
        columns = slice(c * BLOCK, (c + 1) * BLOCK)
        squares = pieces[c] * pieces[c]
        grown = accum_here[:, columns] + squares
        new_accum[:, columns] = grown
        adagrad_total = adagrad_total + jnp.sum(squares / grown, keepdims=True)

    @pl.when(left_side)
    def _():
        rows = product(split(iterate[upper, :]), split(block[...]))
        left_sent.wait_send()
        right_sent.wait_recv()
        precond[...] = product(split(rows), split(root_other[...]))

    @pl.when(right_side)
    def _():
        columns = product(split(block[...]), split(iterate[...]))
        right_sent.wait_send()
        left_sent.wait_recv()
        precond[...] = product(split(root_other[upper, :]), split(columns))

    precond_total = jnp.sum(precond[...] * precond[...], keepdims=True)
    sums[...] = jnp.where(
        lax.broadcasted_iota(jnp.int32, sums.shape, 0) == 0, adagrad_total, precond_total
    )

    swap = remote(precond, other_block, swap_sem.at[0], swap_sem.at[1], swap_peer)

    @pl.when(swapped)
    def _():
        swap.start()

    def reduce_over(peers, source, slots, sends, recvs):
        copies = [
            remote(source, slots.at[j], sends.at[j], recvs.at[j], peer) for j, peer in enumerate(peers)
        ]
        for copy in copies:
            copy.start()
        total = source[...]
        for j, copy in enumerate(copies):
            copy.wait_recv()
            total = total + slots[j]
        return total, copies

    total, sent_mp = reduce_over(mp_peers, sums, mp_sums, mp_send, mp_recv)
    mp_total[...] = total
    total, sent_y = reduce_over(y_peers, mp_total, y_sums, ys_send, ys_recv)
    y_total[...] = total
    total, sent_z = reduce_over(z_peers, y_total, z_sums, zs_send, zs_recv)
    scale = jnp.sqrt(total[0:1, 0:1] / (total[1:2, 0:1] + 1e-12))

    @pl.when(swapped)
    def _():
        swap.wait()
        shard[...] = (other_block[...] * scale).astype(jnp.bfloat16)

    @pl.when(straight)
    def _():
        shard[...] = (precond[...] * scale).astype(jnp.bfloat16)

    first_row, row_count = (0, ROWS_A), (ROWS_A, ROWS_B)

    def region(part):
        kind, (a, b), half = part
        row, depth = wrap(y + a, NY), wrap(z + b, NZ)
        count = row_count[kind]
        begin = row * 1024 + depth // 4 * BLOCK + depth % 2 * HALF + first_row[kind]
        if half is not None:
            count //= 2
            begin = begin + half * count
        column = pl.multiple_of((depth // 2) % 2 * BLOCK, BLOCK)
        return out.at[pl.ds(pl.multiple_of(begin, 16), count), pl.ds(column, BLOCK)]

    start, events = spread_schedule()
    keys = [part for part, _ in events]
    sent = []

    def send(axis, sign, moved):
        kind, offsets, half = moved
        mine = list(offsets)
        mine[axis] += sign
        if offsets[axis] == (NY, NZ)[axis] // 2:
            mine[axis] = sign * offsets[axis] * -1 + sign
        mine = tuple(mine)
        here = region((kind, mine, half))
        if mine == (0, 0):
            count = row_count[kind] // (1 if half is None else 2)
            source = shard.at[pl.ds(first_row[kind] + (half or 0) * count, count), :]
        else:
            source = here
        target = (
            device(x, wrap(y + sign, NY), z, core) if axis == 0 else device(x, y, wrap(z + sign, NZ), core)
        )
        index = keys.index(moved)
        copy = remote(source, here, send_sem.at[index], recv_sem.at[index], target)
        copy.start()
        sent.append(copy)

    for one in start:
        send(*one)
    whole = pltpu.make_async_copy(
        shard,
        out.at[
            pl.ds(pl.multiple_of(y * 1024 + z // 4 * BLOCK + z % 2 * HALF, HALF), HALF),
            pl.ds(pl.multiple_of((z // 2) % 2 * BLOCK, BLOCK), BLOCK),
        ],
        local_sem.at[0],
    )
    whole.start()
    for index, (part, onward) in enumerate(events):
        here = region(part)
        remote(here, here, send_sem.at[index], recv_sem.at[index], swap_peer).wait_recv()
        for one in onward:
            send(*one)
    for copy in gather_sends + sent + sent_mp + sent_y + sent_z:
        copy.wait_send()
    gather_finish()
    whole.wait()

    @pl.when(swapped)
    def _():
        stat_back.wait()

    @pl.when(straight)
    def _():
        for copy in piece_copies:
            copy.wait_send()


def take_step(features, upstream, stats, accum):
    dma = pltpu.SemaphoreType.DMA
    tile = (8, 128)
    count = len(spread_schedule()[1])
    square = pltpu.VMEM((BLOCK, BLOCK), jnp.float32)
    vmem = pl.BlockSpec(memory_space=pltpu.VMEM)
    return pl.pallas_call(
        step_kernel,
        out_shape=(
            pltpu.VMEM((NY * NZ * 128, 1024), jnp.bfloat16),
            pltpu.VMEM((BLOCK, BLOCK), jnp.float32),
            pltpu.VMEM(accum.shape, jnp.float32),
        ),
        in_specs=[pl.BlockSpec(memory_space=pltpu.HBM)] * 4,
        out_specs=(vmem, vmem, vmem),
        scratch_shapes=[
            pltpu.VMEM((NZ, NY, NX, 16, BLOCK), jnp.bfloat16),
            pltpu.VMEM((NZ, NY, 64, BLOCK), jnp.bfloat16),
            pltpu.VMEM((NY, 16, 1024), jnp.bfloat16),
            pltpu.VMEM(accum.shape, jnp.float32),
            square, square, square, square, square, square, square, square,
            pltpu.VMEM((2, 128, BLOCK), jnp.float32),
            pltpu.VMEM((HALF, BLOCK), jnp.float32),
            pltpu.VMEM(tile, jnp.float32),
            pltpu.VMEM((HALF, BLOCK), jnp.float32),
            pltpu.VMEM((HALF, BLOCK), jnp.bfloat16),
            pltpu.VMEM((NX * NC, *tile), jnp.float32),
            pltpu.VMEM((NY, *tile), jnp.float32),
            pltpu.VMEM((NZ, *tile), jnp.float32),
            pltpu.VMEM(tile, jnp.float32),
            pltpu.VMEM(tile, jnp.float32),
            dma((NY,)), dma((NY,)), dma((NZ + 2,)), dma((NZ,)), dma((NZ, 4)), dma((NZ, 4)),
            dma((4, NC)), dma((NZ,)), dma((NZ, 4)), dma((NZ, 4)), dma((3,)),
            dma((2,)), dma((4,)), dma((4,)), dma((2,)), dma((4,)), dma((2,)), dma((2,)), dma((2,)),
            dma((NX * NC,)), dma((NX * NC,)), dma((NY,)), dma((NY,)), dma((NZ,)), dma((NZ,)),
            dma((2,)), dma((count,)), dma((count,)), dma((1,)),
        ],
        compiler_params=pltpu.CompilerParams(
            collective_id=0, has_side_effects=True, vmem_limit_bytes=50 * 2**20
        ),
    )(features, upstream, stats, accum)


def deliver_kernel(update, stat, accum, update_out, stat_out, accum_out, sems):
    copies = []

    def go(source, into):
        copy = pltpu.make_async_copy(source, into, sems.at[len(copies)])
        copy.start()
        copies.append(copy)

    for part in range(8):
        rows = pl.ds(part * 512, 512)
        go(update.at[rows, :], update_out.at[rows, :])
    go(stat, stat_out)
    go(accum, accum_out)
    for copy in copies:
        copy.wait()


def deliver(update, stat, accum):
    return pl.pallas_call(
        deliver_kernel,
        out_shape=tuple(jax.ShapeDtypeStruct(one.shape, one.dtype) for one in (update, stat, accum)),
        in_specs=[pl.BlockSpec(memory_space=pl.ANY)] * 3,
        out_specs=(pl.BlockSpec(memory_space=pltpu.HBM),) * 3,
        scratch_shapes=[pltpu.SemaphoreType.DMA((10,))],
        compiler_params=pltpu.CompilerParams(vmem_limit_bytes=2**20),
    )(update, stat, accum)


def shards(features, upstream, stats, accum):
    update, new_stat, new_accum = deliver(*take_step(features, upstream, stats[0, 0], accum))
    return (new_stat[None, None], new_accum, update)


def solution(mesh):
    placed = (P("dp", None), P("dp", "mp"), P("dp", "mp", None, None), P("dp", "mp"))
    return jax.shard_map(
        shards,
        mesh=mesh,
        in_specs=placed,
        out_specs=(P("dp", "mp", None, None), P("dp", "mp"), P(None, "mp")),
        check_vma=False,
    )
```
